32 devices in a mesh: blk: 8 (over z, x), layer: 4 (over y, core).
Axes of the slice: x: 2, y: 2, z: 4, core: 2. Of those that a mesh axis runs over, the one named last changes fastest.
Arguments:
- tile_values: bfloat16 [16, 4, 1, 128, 128], P('blk', 'layer'), may hold values from 0 to 10, as said below
- band_rows: int32 [16, 4, 1], P('blk', 'layer'), may hold values from 0 to 3, as said below
- kept_rows: int32 [16, 4, 4], P('blk', 'layer'), may hold values from 0 to 3, as said below
- prune_mask: int32 [16, 4, 128], P('blk'), may hold values 0 or 1
Outputs:
- kept: bfloat16 [16, 4, 4, 128, 128], P('blk', None, 'layer')
The draws below stay inside these ranges and needn't reach their ends.
Inputs may be any that keep to these rules, and one draw needn't show every extreme that they name: `tile_values`: positive tile entries. `band_rows`: within each column panel and band the 1 block rows are distinct. `kept_rows`: within each column panel and band the 4 kept block rows are distinct.
All inputs are finite; a program needn't handle non-finite values. No bound on the sum of `prune_mask` on one device may be relied on, other than what follows from the above.
Results may differ from the reference program's by a relative error of at most 0.001.
Values may be sent and summed in bfloat16 or wider, within the bound.
A program may use at most 192 MiB of HBM per device.

```python
import math
import jax
import jax.numpy as jnp

TILE = 128
NB = 16
NQ = 4
RQ = 4
KQ = 1
KOQ = 4


def pattern_of(key):
    inner = jax.random.fold_in(key, 11)
    subkeys = jax.random.split(inner, NB * NQ)
    orders = jax.vmap(lambda one: jax.random.permutation(one, RQ))(subkeys)
    return orders[:, :KQ].reshape(NB, NQ, KQ).astype(jnp.int32)


def draw_band_rows(key, part):
    pattern = pattern_of(key)
    return pattern


def draw_tile_values(key, part):
    pattern = pattern_of(key)
    key = jax.random.fold_in(key, 5)
    scale_key, base_key = jax.random.split(key)
    band_ids = jnp.arange(NQ, dtype=jnp.float32)
    growth = jnp.sqrt(1.0 + 2.0 * band_ids / max(NQ - 1, 1))
    row_power = jax.random.uniform(scale_key, (NQ, RQ, TILE))
    chosen = row_power[jnp.arange(NQ)[None, :, None], pattern]
    row_scale = jnp.power(10.0, 0.5 * chosen)
    shape = (NB, NQ, KQ, TILE, TILE)
    magnitude = jnp.exp(-math.log(1000.0) * jax.random.uniform(base_key, shape))
    values = magnitude * row_scale[..., None] * growth[None, :, None, None, None]
    return values.astype(jnp.bfloat16)


def draw_kept_rows(key, part):
    key = jax.random.fold_in(key, 7)
    subkeys = jax.random.split(key, NB * NQ)
    orders = jax.vmap(lambda one: jax.random.permutation(one, RQ))(subkeys)
    return orders[:, :KOQ].reshape(NB, NQ, KOQ).astype(jnp.int32)


def plant(result, stream_key, smallest, top_value):
    dims = result.shape
    spot = [jax.random.randint(jax.random.fold_in(stream_key, axis), (), 0, dims[axis]) for axis in range(len(dims))]
    result = result.at[tuple(spot)].set(smallest)
    longest = dims.index(max(dims))
    spot[longest] = (spot[longest] + 1) % dims[longest]
    return result.at[tuple(spot)].set(top_value)


def setup_inputs(seed: int = 0) -> dict:
    key_of = jax.random.split(jax.random.key(seed), 5)
    tile_values = draw_tile_values(jax.random.fold_in(key_of[4], 71), 0)
    band_rows = draw_band_rows(jax.random.fold_in(key_of[4], 71), 0)
    kept_rows = draw_kept_rows(jax.random.fold_in(key_of[4], 71), 0)
    prune_mask = plant((jax.random.randint(key_of[3], (NB, NQ, TILE), 0, 4) < 3).astype(jnp.int32), jax.random.fold_in(key_of[3], 1), 0, 1)
    return {"tile_values": tile_values, "band_rows": band_rows, "kept_rows": kept_rows, "prune_mask": prune_mask}


def reference(tile_values, band_rows, kept_rows, prune_mask):
    row_count = NB * TILE
    panel_ids = jnp.arange(NB, dtype=jnp.int32)[:, None, None]
    band_ids = jnp.arange(NQ, dtype=jnp.int32)[None, :, None]
    block_ids = band_ids * RQ + band_rows
    tiled = jnp.zeros((NB, NB, TILE, TILE), jnp.bfloat16)
    tiled = tiled.at[block_ids, jnp.broadcast_to(panel_ids, block_ids.shape)].set(tile_values)
    matrix = tiled.transpose(0, 2, 1, 3).reshape(row_count, row_count)
    expanded = jnp.dot(matrix, matrix, preferred_element_type=jnp.float32)
    squared = expanded * expanded
    totals = jnp.sum(squared, axis=0)
    scaled = (squared * (row_count / totals)).astype(jnp.bfloat16)
    blocked = scaled.reshape(NB, TILE, NB, TILE)
    kept_blocks = band_ids * RQ + kept_rows
    picked = blocked[kept_blocks, :, jnp.broadcast_to(panel_ids, kept_blocks.shape), :]
    keep_mask = prune_mask[:, :, None, None, :].astype(jnp.bfloat16)
    return picked * keep_mask
```

```python
import functools

import jax
import jax.numpy as jnp
from jax import lax
from jax.experimental import pallas as pl
from jax.experimental.pallas import tpu as pltpu
from jax.sharding import PartitionSpec as P

MESH = pl.DeviceIdType.MESH
NOTE = 16


def each(count, body, most=8):
    if count <= most:
        for i in range(count):
            body(i)
    else:
        lax.fori_loop(0, count, lambda i, carry: (body(i), carry)[1], 0)


def kernel(
    cycle, bands, tiles_ref, rows_ref, kept_ref, mask_ref, out_ref,
    left, right, expanded, totals, stage,
    line_send, pair_send, layer_send, left_recv, right_recv,
    total_send, total_recv, out_send, out_recv,
):
    panels, per_band, tile = tiles_ref.shape[0], tiles_ref.shape[2], tiles_ref.shape[3]
    per_layer = out_ref.shape[2]
    count = panels * per_band
    body = count * tile
    band_blocks = panels * cycle // bands
    owners = band_blocks // panels
    me, layer = lax.axis_index("blk"), lax.axis_index("layer")
    half = cycle // 2
    pair = me + 1 - 2 * lax.rem(me, 2)
    line = [lax.rem(me + 2 * s, cycle) for s in range(1, half)]
    sources = [lax.rem(me + cycle - 2 * s, cycle) for s in range(1, half)]
    others = [lax.rem(layer + s, bands) for s in range(1, bands)]
    other_sources = [lax.rem(layer + bands - s, bands) for s in range(1, bands)]

    barrier = pltpu.get_barrier_semaphore()
    for peer in line + [pair]:
        pl.semaphore_signal(barrier, inc=1, device_id={"blk": peer}, device_id_type=MESH)
    for peer in others:
        pl.semaphore_signal(barrier, inc=1, device_id={"layer": peer}, device_id_type=MESH)

    row_ids = lax.broadcasted_iota(jnp.int32, (NOTE, tile), 0)
    note = jnp.zeros((NOTE, tile), jnp.float32)
    for j in range(panels):
        for k in range(per_band):
            at = j * per_band + k
            left[me, at * tile:(at + 1) * tile, :] = tiles_ref[j, 0, k]
            note = jnp.where(row_ids == at, rows_ref[j, 0, k].astype(jnp.float32), note)
    left[me, body:body + NOTE, :] = note.astype(jnp.bfloat16)

    pl.semaphore_wait(barrier, len(line) + 1 + len(others))

    def send_left(slot, target, send_sem):
        return pltpu.make_async_remote_copy(
            src_ref=left.at[slot], dst_ref=left.at[slot], send_sem=send_sem,
            recv_sem=left_recv.at[slot], device_id={"blk": target}, device_id_type=MESH,
        )

    copies = []
    for s, peer in enumerate(line):
        copies.append(send_left(me, peer, line_send.at[s]))
    copies.append(send_left(me, pair, pair_send.at[0]))
    for s, peer in enumerate(others):
        copies.append(pltpu.make_async_remote_copy(
            src_ref=left.at[me], dst_ref=right.at[layer], send_sem=layer_send.at[s],
            recv_sem=right_recv.at[layer], device_id={"layer": peer}, device_id_type=MESH,
        ))
    for copy in copies:
        copy.start()
    right[layer] = left[me]

    for s, source in enumerate(sources):
        send_left(source, pair, pair_send.at[0]).wait_recv()
        onward = send_left(source, pair, pair_send.at[s + 1])
        onward.start()
        copies.append(onward)
    send_left(pair, pair, pair_send.at[0]).wait_recv()
    for source in sources:
        twin = source + 1 - 2 * lax.rem(source, 2)
        send_left(twin, pair, pair_send.at[0]).wait_recv()
    for source in other_sources:
        pltpu.make_async_remote_copy(
            src_ref=left.at[me], dst_ref=right.at[source], send_sem=layer_send.at[0],
            recv_sem=right_recv.at[source], device_id={"layer": others[0]}, device_id_type=MESH,
        ).wait_recv()

    for p in range(panels):
        for b in range(band_blocks):
            expanded[p, b] = jnp.zeros((tile, tile), jnp.float32)

        def product(q, p=p):
            wanted = right[q, body:body + NOTE, :].astype(jnp.float32)
            for k in range(per_band):
                at = p * per_band + k
                want = wanted[at:at + 1]
                factor = right[q, at * tile:(at + 1) * tile, :]
                for kk in range(per_band):

                    def choose(o, carry):
                        block, landing = carry
                        owner = q * owners + o
                        notes = left[owner, body:body + NOTE, :].astype(jnp.float32)
                        for j in range(panels):
                            t = j * per_band + kk
                            r = jnp.asarray(o * panels + j).astype(jnp.float32)
                            pick = jnp.where(want == r, 1.0, 0.0)
                            block = block + left[owner, t * tile:(t + 1) * tile, :] * pick.astype(jnp.bfloat16)
                            landing = landing + notes[t:t + 1] * pick
                        return block, landing

                    carry = jnp.zeros((tile, tile), jnp.bfloat16), jnp.zeros((1, tile), jnp.float32)
                    if owners <= 4:
                        for o in range(owners):
                            carry = choose(o, carry)
                    else:
                        carry = lax.fori_loop(0, owners, choose, carry)
                    block, landing = carry
                    term = jnp.dot(block, factor, preferred_element_type=jnp.float32)

                    def land(b):
                        here = landing == jnp.asarray(b).astype(jnp.float32)
                        expanded[p, b] += jnp.where(here, term, 0.0)

                    each(band_blocks, land, 4)

        each(bands, product, 4 if per_band == 1 else 0)

        partial = jnp.zeros((1, tile), jnp.float32)
        for b in range(band_blocks):
            values = expanded[p, b]
            partial = partial + jnp.sum(values * values, axis=0, keepdims=True)
        totals[layer, p] = jnp.broadcast_to(partial, (8, tile))

    def send_total(s, peer, slot):
        return pltpu.make_async_remote_copy(
            src_ref=totals.at[slot], dst_ref=totals.at[slot], send_sem=total_send.at[s],
            recv_sem=total_recv.at[slot], device_id={"layer": peer}, device_id_type=MESH,
        )

    for s, peer in enumerate(others):
        copy = send_total(s, peer, layer)
        copy.start()
        copies.append(copy)
    for source in other_sources:
        send_total(0, others[0], source).wait_recv()

    row_count = float(panels * cycle * tile)
    factors = []
    for p in range(panels):
        total = totals[0, p]
        for q in range(1, bands):
            total = total + totals[q, p]
        keep = mask_ref[p, pl.ds(layer, 1), :].astype(jnp.float32)
        factors.append((row_count / total[0:1], keep))

    def block_of(p, m, j):
        scale, keep = factors[p]
        values = expanded[p, kept_ref[p, 0, m * per_layer + j]]
        return (values * values * scale * keep).astype(jnp.bfloat16)

    def send_out(s, peer, band):
        return pltpu.make_async_remote_copy(
            src_ref=stage.at[s], dst_ref=out_ref.at[:, band], send_sem=out_send.at[s],
            recv_sem=out_recv.at[band], device_id={"layer": peer}, device_id_type=MESH,
        )

    for s, peer in enumerate(others):
        for p in range(panels):
            for j in range(per_layer):
                stage[s, p, j] = block_of(p, peer, j)
        copy = send_out(s, peer, layer)
        copy.start()
        copies.append(copy)
    for p in range(panels):
        for j in range(per_layer):
            out_ref[p, layer, j] = block_of(p, layer, j)
    for source in other_sources:
        send_out(0, others[0], source).wait_recv()
    for copy in copies:
        copy.wait_send()


def solution(mesh):
    cycle, bands = mesh.shape["blk"], mesh.shape["layer"]

    def per_device(tile_values, band_rows, kept_rows, prune_mask):
        panels, _, per_band, tile, _ = tile_values.shape
        per_layer = kept_rows.shape[2] // bands
        band_blocks = panels * cycle // bands
        message = panels * per_band * tile + NOTE
        dma = pltpu.SemaphoreType.DMA
        vmem = pl.BlockSpec(memory_space=pltpu.VMEM)
        smem = pl.BlockSpec(memory_space=pltpu.SMEM)
        return pl.pallas_call(
            functools.partial(kernel, cycle, bands),
            out_shape=jax.ShapeDtypeStruct((panels, bands, per_layer, tile, tile), jnp.bfloat16),
            in_specs=[vmem, smem, smem, vmem],
            out_specs=vmem,
            scratch_shapes=[
                pltpu.VMEM((cycle, message, tile), jnp.bfloat16),
                pltpu.VMEM((bands, message, tile), jnp.bfloat16),
                pltpu.VMEM((panels, band_blocks, tile, tile), jnp.float32),
                pltpu.VMEM((bands, panels, 8, tile), jnp.float32),
                pltpu.VMEM((bands - 1, panels, per_layer, tile, tile), jnp.bfloat16),
                dma((cycle // 2,)),
                dma((cycle // 2,)),
                dma((bands,)),
                dma((cycle,)),
                dma((bands,)),
                dma((bands,)),
                dma((bands,)),
                dma((bands,)),
                dma((bands,)),
            ],
            compiler_params=pltpu.CompilerParams(
                collective_id=0, has_side_effects=True, vmem_limit_bytes=32 * 1024 * 1024
            ),
        )(tile_values, band_rows, kept_rows, prune_mask)

    return jax.shard_map(
        per_device,
        mesh=mesh,
        in_specs=(
            P("blk", "layer", None, None, None),
            P("blk", "layer", None),
            P("blk", "layer", None),
            P("blk", None, None),
        ),
        out_specs=P("blk", None, "layer", None, None),
        check_vma=False,
    )
```

```python
import functools

import jax
import jax.numpy as jnp
from jax import lax
from jax.experimental import pallas as pl
from jax.experimental.pallas import tpu as pltpu
from jax.sharding import PartitionSpec as P

MESH = pl.DeviceIdType.MESH
NOTE = 16


def each(count, body, most=8):
    if count <= most:
        for i in range(count):
            body(i)
    else:
        lax.fori_loop(0, count, lambda i, carry: (body(i), carry)[1], 0)


def xor(a, c):
    result, bit = a, 1
    while bit <= c:
        if c // bit % 2:
            result = result + bit * (1 - 2 * lax.rem(a // bit, 2))
        bit *= 2
    return result


def kernel(
    cycle, bands, panels, per_band, tiles_hbm, rows_hbm, kept_hbm, mask_hbm, out_ref,
    left, right, expanded, totals, stage, rows_ref, kept_ref, mask_ref,
    local, line_send, pair_send, layer_send, left_recv, right_recv,
    total_send, total_recv, out_send, out_recv, keep_sem,
):
    tile = tiles_hbm.shape[1]
    per_layer = out_ref.shape[2]
    count = panels * per_band
    body = count * tile
    band_blocks = panels * cycle // bands
    owners = band_blocks // panels
    lanes = owners // 2
    me, layer = lax.axis_index("blk"), lax.axis_index("layer")
    side = lax.rem(me, 2)
    pair = me + 1 - 2 * side
    mine = me // 2
    own_band, own_lane = mine // lanes, lax.rem(mine, lanes)
    others = [lax.rem(layer + s, bands) for s in range(1, bands)]

    def owners_of(d, which):
        band = xor(own_band, d)
        return [2 * (band * lanes + lax.rem(own_lane + h, lanes)) + which for h in range(lanes)]

    line = [owners_of(d, side) for d in range(bands)]
    line[0] = line[0][1:]
    targets = []
    for d in range(bands):
        band = xor(own_band, d)
        for h in range(lanes):
            if d or h:
                targets.append(2 * (band * lanes + lax.rem(own_lane + lanes - h, lanes)) + side)

    fetch_rows = pltpu.make_async_copy(rows_hbm, rows_ref, local.at[0])
    fetch_tiles = pltpu.make_async_copy(tiles_hbm, left.at[me, pl.ds(0, body)], local.at[1])
    fetch_right = pltpu.make_async_copy(tiles_hbm, right.at[layer, pl.ds(0, body)], local.at[2])
    fetch_kept = pltpu.make_async_copy(kept_hbm, kept_ref, local.at[3])
    fetch_mask = pltpu.make_async_copy(mask_hbm, mask_ref, local.at[4])
    for fetch in (fetch_rows, fetch_tiles, fetch_right, fetch_kept, fetch_mask):
        fetch.start()

    barrier = pltpu.get_barrier_semaphore()
    for peer in targets + [pair]:
        pl.semaphore_signal(barrier, inc=1, device_id={"blk": peer}, device_id_type=MESH)
    for peer in others:
        pl.semaphore_signal(barrier, inc=1, device_id={"layer": peer}, device_id_type=MESH)

    fetch_rows.wait()
    row_ids = lax.broadcasted_iota(jnp.int32, (NOTE, tile), 0)
    note = jnp.zeros((NOTE, tile), jnp.float32)
    for j in range(panels):
        for k in range(per_band):
            note = jnp.where(row_ids == j * per_band + k, rows_ref[0, k, j].astype(jnp.float32), note)
    note = note.astype(jnp.bfloat16)
    left[me, body:body + NOTE, :] = note
    right[layer, body:body + NOTE, :] = note
    fetch_tiles.wait()

    pl.semaphore_wait(barrier, len(targets) + 1 + len(others))

    def send_left(slot, target, send_sem):
        return pltpu.make_async_remote_copy(
            src_ref=left.at[slot], dst_ref=left.at[slot], send_sem=send_sem,
            recv_sem=left_recv.at[slot], device_id={"blk": target}, device_id_type=MESH,
        )

    def send_right(s, peer, band):
        return pltpu.make_async_remote_copy(
            src_ref=left.at[me], dst_ref=right.at[band], send_sem=layer_send.at[s],
            recv_sem=right_recv.at[band], device_id={"layer": peer}, device_id_type=MESH,
        )

    copies = [send_left(me, pair, pair_send.at[0])]
    for s, peer in enumerate(targets):
        copies.append(send_left(me, peer, line_send.at[s]))
    for s, peer in enumerate(others):
        copies.append(send_right(s, peer, layer))
    for copy in copies:
        copy.start()

    def forward(d):
        for source in line[d]:
            send_left(source, pair, pair_send.at[0]).wait_recv()
            onward = send_left(source, pair, pair_send.at[len(copies) - len(targets) - len(others)])
            onward.start()
            copies.append(onward)

    def product(d, p):
        q = xor(own_band, d)
        wanted = right[q, body:body + NOTE, :].astype(jnp.float32)
        for k in range(per_band):
            at = p * per_band + k
            want = wanted[at:at + 1]
            factor = right[q, at * tile:(at + 1) * tile, :]
            for kk in range(per_band):

                def choose(o, carry):
                    block, landing = carry
                    owner = q * owners + o
                    notes = left[owner, body:body + NOTE, :].astype(jnp.float32)
                    for j in range(panels):
                        t = j * per_band + kk
                        r = jnp.asarray(o * panels + j).astype(jnp.float32)
                        pick = jnp.where(want == r, 1.0, 0.0)
                        block = block + left[owner, t * tile:(t + 1) * tile, :] * pick.astype(jnp.bfloat16)
                        landing = landing + notes[t:t + 1] * pick
                    return block, landing

                carry = jnp.zeros((tile, tile), jnp.bfloat16), jnp.zeros((1, tile), jnp.float32)
                if owners <= 4:
                    for o in range(owners):
                        carry = choose(o, carry)
                else:
                    carry = lax.fori_loop(0, owners, choose, carry)
                block, landing = carry
                term = jnp.dot(block, factor, preferred_element_type=jnp.float32)

                def land(b):
                    here = landing == jnp.asarray(b).astype(jnp.float32)
                    value = jnp.where(here, term, 0.0)
                    if d or k or kk:
                        value = expanded[p, b] + value
                    expanded[p, b] = value

                each(band_blocks, land, 4)

    def arrive(d):
        for twin in owners_of(d, 1 - side):
            send_left(twin, pair, pair_send.at[0]).wait_recv()

    def send_total(s, peer, slot, p):
        return pltpu.make_async_remote_copy(
            src_ref=totals.at[slot, p], dst_ref=totals.at[slot, p], send_sem=total_send.at[s, p],
            recv_sem=total_recv.at[slot, p], device_id={"layer": peer}, device_id_type=MESH,
        )

    forward(0)
    forward(1)
    fetch_right.wait()
    for s, peer in enumerate(others):
        send_right(s, peer, peer).wait_recv()
    for d in range(bands):
        arrive(d)
        last = d == bands - 1
        for p in range(panels):
            product(d, p)
            if last:
                partial = jnp.zeros((1, tile), jnp.float32)
                for b in range(band_blocks):
                    values = expanded[p, b]
                    partial = partial + jnp.sum(values * values, axis=0, keepdims=True)
                totals[layer, p] = jnp.broadcast_to(partial, (8, tile))
                for s, peer in enumerate(others):
                    copy = send_total(s, peer, layer, p)
                    copy.start()
                    copies.append(copy)
        if d + 2 < bands:
            forward(d + 2)

    row_count = float(panels * cycle * tile)
    fetch_kept.wait()
    fetch_mask.wait()

    def send_out(s, peer, band, p):
        return pltpu.make_async_remote_copy(
            src_ref=stage.at[s, p], dst_ref=out_ref.at[p, band], send_sem=out_send.at[s, p],
            recv_sem=out_recv.at[band, p], device_id={"layer": peer}, device_id_type=MESH,
        )

    keeps = []
    for p in range(panels):
        for s, source in enumerate(others):
            send_total(s, source, source, p).wait_recv()
        total = totals[0, p]
        for q in range(1, bands):
            total = total + totals[q, p]
        scale = row_count / total[0:1]
        keep = mask_ref[p, pl.ds(layer, 1), :].astype(jnp.float32)

        def block_of(m, j):
            values = expanded[p, kept_ref[p, 0, m * per_layer + j]]
            return (values * values * scale * keep).astype(jnp.bfloat16)

        for s, peer in enumerate(others):
            for j in range(per_layer):
                stage[s, p, j] = block_of(peer, j)
            copy = send_out(s, peer, layer, p)
            copy.start()
            copies.append(copy)
        for j in range(per_layer):
            stage[bands - 1, p, j] = block_of(layer, j)
        keeps.append(pltpu.make_async_copy(stage.at[bands - 1, p], out_ref.at[p, layer], keep_sem.at[p]))
        keeps[-1].start()
    for p in range(panels):
        for s, source in enumerate(others):
            send_out(s, source, source, p).wait_recv()
    for copy in keeps:
        copy.wait()
    for copy in copies:
        copy.wait_send()


def solution(mesh):
    cycle, bands = mesh.shape["blk"], mesh.shape["layer"]

    def per_device(tile_values, band_rows, kept_rows, prune_mask):
        panels, _, per_band, tile, _ = tile_values.shape
        per_layer = kept_rows.shape[2] // bands
        band_blocks = panels * cycle // bands
        message = panels * per_band * tile + NOTE
        dma = pltpu.SemaphoreType.DMA
        hbm = pl.BlockSpec(memory_space=pltpu.HBM)
        return pl.pallas_call(
            functools.partial(kernel, cycle, bands, panels, per_band),
            out_shape=jax.ShapeDtypeStruct((panels, bands, per_layer, tile, tile), jnp.bfloat16),
            in_specs=[hbm] * 4,
            out_specs=hbm,
            scratch_shapes=[
                pltpu.VMEM((cycle, message, tile), jnp.bfloat16),
                pltpu.VMEM((bands, message, tile), jnp.bfloat16),
                pltpu.VMEM((panels, band_blocks, tile, tile), jnp.float32),
                pltpu.VMEM((bands, panels, 8, tile), jnp.float32),
                pltpu.VMEM((bands, panels, per_layer, tile, tile), jnp.bfloat16),
                pltpu.SMEM((1, per_band, panels), jnp.int32),
                pltpu.SMEM(kept_rows.shape, jnp.int32),
                pltpu.VMEM(prune_mask.shape, jnp.int32),
                dma((5,)),
                dma((cycle // 2,)),
                dma((cycle // 2,)),
                dma((bands,)),
                dma((cycle,)),
                dma((bands,)),
                dma((bands, panels)),
                dma((bands, panels)),
                dma((bands, panels)),
                dma((bands, panels)),
                dma((panels,)),
            ],
            compiler_params=pltpu.CompilerParams(
                collective_id=0, has_side_effects=True, vmem_limit_bytes=63 * 1024 * 1024
            ),
        )(
            tile_values.reshape(panels * per_band * tile, tile),
            band_rows.transpose(1, 2, 0),
            kept_rows,
            prune_mask,
        )

    return jax.shard_map(
        per_device,
        mesh=mesh,
        in_specs=(
            P("blk", "layer", None, None, None),
            P("blk", "layer", None),
            P("blk", "layer", None),
            P("blk", None, None),
        ),
        out_specs=P("blk", None, "layer", None, None),
        check_vma=False,
    )
```

```python
import functools

import jax
import jax.numpy as jnp
from jax import lax
from jax.experimental import pallas as pl
from jax.experimental.pallas import tpu as pltpu
from jax.sharding import PartitionSpec as P

MESH = pl.DeviceIdType.MESH
NOTE = 16


def each(count, body, most=8):
    if count <= most:
        for i in range(count):
            body(i)
    else:
        lax.fori_loop(0, count, lambda i, carry: (body(i), carry)[1], 0)


def xor(a, c):
    result, bit = a, 1
    while bit <= c:
        if c // bit % 2:
            result = result + bit * (1 - 2 * lax.rem(a // bit, 2))
        bit *= 2
    return result


def kernel(
    cycle, bands, panels, per_band, tiles_hbm, rows_hbm, kept_hbm, mask_hbm, out_ref,
    left, right, expanded, totals, stage, rows_ref, kept_ref, mask_ref,
    local, line_send, pair_send, layer_send, left_recv, right_recv,
    total_send, total_recv, out_send, out_recv, keep_sem,
):
    tile = tiles_hbm.shape[1]
    per_layer = out_ref.shape[2]
    count = panels * per_band
    body = count * tile
    band_blocks = panels * cycle // bands
    owners = band_blocks // panels
    lanes = owners // 2
    me, layer = lax.axis_index("blk"), lax.axis_index("layer")
    side = lax.rem(me, 2)
    pair = me + 1 - 2 * side
    mine = me // 2
    own_band, own_lane = mine // lanes, lax.rem(mine, lanes)
    others = [lax.rem(layer + s, bands) for s in range(1, bands)]

    def owners_of(d, which):
        band = xor(own_band, d)
        return [2 * (band * lanes + lax.rem(own_lane + h, lanes)) + which for h in range(lanes)]

    line = [owners_of(d, side) for d in range(bands)]
    line[0] = line[0][1:]
    targets = []
    for d in range(bands):
        band = xor(own_band, d)
        for h in range(lanes):
            if d or h:
                targets.append(2 * (band * lanes + lax.rem(own_lane + lanes - h, lanes)) + side)

    fetch_rows = pltpu.make_async_copy(rows_hbm, rows_ref, local.at[0])
    fetch_tiles = pltpu.make_async_copy(tiles_hbm, left.at[me, pl.ds(NOTE, body)], local.at[1])
    fetch_right = pltpu.make_async_copy(tiles_hbm, right.at[layer, pl.ds(NOTE, body)], local.at[2])
    fetch_kept = pltpu.make_async_copy(kept_hbm, kept_ref, local.at[3])
    fetch_mask = pltpu.make_async_copy(mask_hbm, mask_ref, local.at[4])
    for fetch in (fetch_rows, fetch_tiles, fetch_right, fetch_kept, fetch_mask):
        fetch.start()

    barrier = pltpu.get_barrier_semaphore()
    for peer in targets + [pair]:
        pl.semaphore_signal(barrier, inc=1, device_id={"blk": peer}, device_id_type=MESH)
    for peer in others:
        pl.semaphore_signal(barrier, inc=1, device_id={"layer": peer}, device_id_type=MESH)

    fetch_rows.wait()
    row_ids = lax.broadcasted_iota(jnp.int32, (NOTE, tile), 0)
    note = jnp.zeros((NOTE, tile), jnp.float32)
    for j in range(panels):
        for k in range(per_band):
            note = jnp.where(row_ids == j * per_band + k, rows_ref[0, k, j].astype(jnp.float32), note)
    note = note.astype(jnp.bfloat16)
    left[me, 0:NOTE, :] = note
    right[layer, 0:NOTE, :] = note
    fetch_tiles.wait()

    pl.semaphore_wait(barrier, len(targets) + 1 + len(others))

    part = per_band * tile
    chunks = [(NOTE + c * part if c else 0, part if c else NOTE + part) for c in range(panels)]

    def send_left(slot, target, send_sem, c):
        rows = pl.ds(*chunks[c])
        return pltpu.make_async_remote_copy(
            src_ref=left.at[slot, rows], dst_ref=left.at[slot, rows], send_sem=send_sem,
            recv_sem=left_recv.at[slot, c], device_id={"blk": target}, device_id_type=MESH,
        )

    def send_right(s, peer, band):
        return pltpu.make_async_remote_copy(
            src_ref=left.at[me], dst_ref=right.at[band], send_sem=layer_send.at[s],
            recv_sem=right_recv.at[band], device_id={"layer": peer}, device_id_type=MESH,
        )

    copies = []
    for c in range(panels):
        copies.append(send_left(me, pair, pair_send.at[0, c], c))
        for s, peer in enumerate(targets):
            copies.append(send_left(me, peer, line_send.at[s, c], c))
    for s, peer in enumerate(others):
        copies.append(send_right(s, peer, layer))
    for copy in copies:
        copy.start()

    sources = [source for band in line for source in band]
    for c in range(panels):
        for s, source in enumerate(sources):
            onward = send_left(source, pair, pair_send.at[s + 1, c], c)
            onward.wait_recv()
            onward.start()
            copies.append(onward)

    def product(d, p):
        q = xor(own_band, d)
        wanted = right[q, 0:NOTE, :].astype(jnp.float32)
        for k in range(per_band):
            at = p * per_band + k
            want = wanted[at:at + 1]
            factor = right[q, NOTE + at * tile:NOTE + (at + 1) * tile, :]
            for kk in range(per_band):

                def choose(o, carry):
                    block, landing = carry
                    owner = q * owners + o
                    notes = left[owner, 0:NOTE, :].astype(jnp.float32)
                    for j in range(panels):
                        t = j * per_band + kk
                        r = jnp.asarray(o * panels + j).astype(jnp.float32)
                        pick = jnp.where(want == r, 1.0, 0.0)
                        block = block + left[owner, NOTE + t * tile:NOTE + (t + 1) * tile, :] * pick.astype(jnp.bfloat16)
                        landing = landing + notes[t:t + 1] * pick
                    return block, landing

                carry = jnp.zeros((tile, tile), jnp.bfloat16), jnp.zeros((1, tile), jnp.float32)
                if owners <= 4:
                    for o in range(owners):
                        carry = choose(o, carry)
                else:
                    carry = lax.fori_loop(0, owners, choose, carry)
                block, landing = carry
                term = jnp.dot(block, factor, preferred_element_type=jnp.float32)

                def land(b):
                    here = landing == jnp.asarray(b).astype(jnp.float32)
                    value = jnp.where(here, term, 0.0)
                    if d or k or kk:
                        value = expanded[p, b] + value
                    expanded[p, b] = value

                each(band_blocks, land, 4)

    def arrive(d):
        for c in range(panels):
            for twin in owners_of(d, 1 - side):
                send_left(twin, pair, pair_send.at[0, c], c).wait_recv()

    def send_total(s, peer, slot, p):
        return pltpu.make_async_remote_copy(
            src_ref=totals.at[slot, p], dst_ref=totals.at[slot, p], send_sem=total_send.at[s, p],
            recv_sem=total_recv.at[slot, p], device_id={"layer": peer}, device_id_type=MESH,
        )

    fetch_right.wait()
    for s, peer in enumerate(others):
        send_right(s, peer, peer).wait_recv()
    for d in range(bands):
        arrive(d)
        last = d == bands - 1
        for p in range(panels):
            product(d, p)
            if last:
                partial = jnp.zeros((1, tile), jnp.float32)
                for b in range(band_blocks):
                    values = expanded[p, b]
                    partial = partial + jnp.sum(values * values, axis=0, keepdims=True)
                totals[layer, p] = jnp.broadcast_to(partial, (8, tile))
                for s, peer in enumerate(others):
                    copy = send_total(s, peer, layer, p)
                    copy.start()
                    copies.append(copy)

    row_count = float(panels * cycle * tile)
    fetch_kept.wait()
    fetch_mask.wait()

    def send_out(s, peer, band, p):
        return pltpu.make_async_remote_copy(
            src_ref=stage.at[s, p], dst_ref=out_ref.at[p, band], send_sem=out_send.at[s, p],
            recv_sem=out_recv.at[band, p], device_id={"layer": peer}, device_id_type=MESH,
        )

    keeps = []
    for p in range(panels):
        for s, source in enumerate(others):
            send_total(s, source, source, p).wait_recv()
        total = totals[0, p]
        for q in range(1, bands):
            total = total + totals[q, p]
        scale = row_count / total[0:1]
        keep = mask_ref[p, pl.ds(layer, 1), :].astype(jnp.float32)

        def block_of(m, j):
            values = expanded[p, kept_ref[p, 0, m * per_layer + j]]
            return (values * values * scale * keep).astype(jnp.bfloat16)

        for s, peer in enumerate(others):
            for j in range(per_layer):
                stage[s, p, j] = block_of(peer, j)
            copy = send_out(s, peer, layer, p)
            copy.start()
            copies.append(copy)
        for j in range(per_layer):
            stage[bands - 1, p, j] = block_of(layer, j)
        keeps.append(pltpu.make_async_copy(stage.at[bands - 1, p], out_ref.at[p, layer], keep_sem.at[p]))
        keeps[-1].start()
    for p in range(panels):
        for s, source in enumerate(others):
            send_out(s, source, source, p).wait_recv()
    for copy in keeps:
        copy.wait()
    for copy in copies:
        copy.wait_send()


def solution(mesh):
    cycle, bands = mesh.shape["blk"], mesh.shape["layer"]

    def per_device(tile_values, band_rows, kept_rows, prune_mask):
        panels, _, per_band, tile, _ = tile_values.shape
        per_layer = kept_rows.shape[2] // bands
        band_blocks = panels * cycle // bands
        message = panels * per_band * tile + NOTE
        dma = pltpu.SemaphoreType.DMA
        hbm = pl.BlockSpec(memory_space=pltpu.HBM)
        return pl.pallas_call(
            functools.partial(kernel, cycle, bands, panels, per_band),
            out_shape=jax.ShapeDtypeStruct((panels, bands, per_layer, tile, tile), jnp.bfloat16),
            in_specs=[hbm] * 4,
            out_specs=hbm,
            scratch_shapes=[
                pltpu.VMEM((cycle, message, tile), jnp.bfloat16),
                pltpu.VMEM((bands, message, tile), jnp.bfloat16),
                pltpu.VMEM((panels, band_blocks, tile, tile), jnp.float32),
                pltpu.VMEM((bands, panels, 8, tile), jnp.float32),
                pltpu.VMEM((bands, panels, per_layer, tile, tile), jnp.bfloat16),
                pltpu.SMEM((1, per_band, panels), jnp.int32),
                pltpu.SMEM(kept_rows.shape, jnp.int32),
                pltpu.VMEM(prune_mask.shape, jnp.int32),
                dma((5,)),
                dma((cycle // 2, panels)),
                dma((cycle // 2, panels)),
                dma((bands,)),
                dma((cycle, panels)),
                dma((bands,)),
                dma((bands, panels)),
                dma((bands, panels)),
                dma((bands, panels)),
                dma((bands, panels)),
                dma((panels,)),
            ],
            compiler_params=pltpu.CompilerParams(
                collective_id=0, has_side_effects=True, vmem_limit_bytes=63 * 1024 * 1024
            ),
        )(
            tile_values.reshape(panels * per_band * tile, tile),
            band_rows.transpose(1, 2, 0),
            kept_rows,
            prune_mask,
        )

    return jax.shard_map(
        per_device,
        mesh=mesh,
        in_specs=(
            P("blk", "layer", None, None, None),
            P("blk", "layer", None),
            P("blk", "layer", None),
            P("blk", None, None),
        ),
        out_specs=P("blk", None, "layer", None, None),
        check_vma=False,
    )
```

```python
import functools

import jax
import jax.numpy as jnp
from jax import lax
from jax.experimental import pallas as pl
from jax.experimental.pallas import tpu as pltpu
from jax.sharding import PartitionSpec as P

MESH = pl.DeviceIdType.MESH
NOTE = 16


def each(count, body):
    lax.fori_loop(0, count, lambda i, carry: (body(i), carry)[1], 0)


def xor(a, c, count):
    result, bit = 0, 1
    while bit < count:
        result = result + bit * lax.rem(a // bit + c // bit, 2)
        bit *= 2
    return result


def kernel(
    cycle, bands, panels, per_band, tiles_hbm, rows_hbm, kept_hbm, mask_hbm, out_ref,
    left, right, expanded, totals, stage, rows_ref, kept_ref, mask_ref,
    local, line_send, pair_send, layer_send, left_recv, right_recv,
    total_send, total_recv, out_send, out_recv, keep_sem,
):
    tile = tiles_hbm.shape[1]
    per_layer = out_ref.shape[2]
    body = panels * per_band * tile
    band_blocks = panels * cycle // bands
    owners = band_blocks // panels
    lanes = owners // 2
    onward = cycle // 2 - 1
    me, layer = lax.axis_index("blk"), lax.axis_index("layer")
    side = lax.rem(me, 2)
    pair = me + 1 - 2 * side
    own_band, own_lane = me // owners, lax.rem(me // 2, lanes)

    def other(s):
        return lax.rem(layer + 1 + s, bands)

    def owner_at(i, which):
        band = xor(own_band, i // lanes, bands)
        return 2 * (band * lanes + lax.rem(own_lane + lax.rem(i, lanes), lanes)) + which

    def target_at(i):
        band = xor(own_band, i // lanes, bands)
        return 2 * (band * lanes + lax.rem(own_lane + lanes - lax.rem(i, lanes), lanes)) + side

    fetch_rows = pltpu.make_async_copy(rows_hbm, rows_ref, local.at[0])
    fetch_tiles = pltpu.make_async_copy(tiles_hbm, left.at[me, pl.ds(NOTE, body)], local.at[1])
    fetch_right = pltpu.make_async_copy(tiles_hbm, right.at[layer, pl.ds(NOTE, body)], local.at[2])
    fetch_kept = pltpu.make_async_copy(kept_hbm, kept_ref, local.at[3])
    fetch_mask = pltpu.make_async_copy(mask_hbm, mask_ref, local.at[4])

    barrier = pltpu.get_barrier_semaphore()

    def greet(peer):
        pl.semaphore_signal(barrier, inc=1, device_id=peer, device_id_type=MESH)

    greet({"blk": pair})
    each(onward, lambda i: greet({"blk": target_at(i + 1)}))
    each(bands - 1, lambda s: greet({"layer": other(s)}))
    for fetch in (fetch_rows, fetch_tiles, fetch_right, fetch_kept, fetch_mask):
        fetch.start()

    fetch_rows.wait()
    row_ids = lax.broadcasted_iota(jnp.int32, (NOTE, tile), 0)
    note = jnp.zeros((NOTE, tile), jnp.float32)
    for j in range(panels):
        for k in range(per_band):
            note = jnp.where(row_ids == j * per_band + k, rows_ref[0, k, j].astype(jnp.float32), note)
    note = note.astype(jnp.bfloat16)
    left[me, 0:NOTE, :] = note
    right[layer, 0:NOTE, :] = note
    fetch_tiles.wait()
    pl.semaphore_wait(barrier, onward + bands)

    part = per_band * tile
    chunks = [(NOTE + c * part if c else 0, part if c else NOTE + part) for c in range(panels)]

    def send_left(slot, target, send_sem, c):
        rows = pl.ds(*chunks[c])
        return pltpu.make_async_remote_copy(
            src_ref=left.at[slot, rows], dst_ref=left.at[slot, rows], send_sem=send_sem,
            recv_sem=left_recv.at[slot, c], device_id={"blk": target}, device_id_type=MESH,
        )

    def send_right(s, band):
        return pltpu.make_async_remote_copy(
            src_ref=left.at[me], dst_ref=right.at[band], send_sem=layer_send.at[s],
            recv_sem=right_recv.at[band], device_id={"layer": other(s)}, device_id_type=MESH,
        )

    def along(i, c):
        return send_left(me, target_at(i + 1), line_send.at[i, c], c)

    def across(i, c):
        return send_left(owner_at(i, side), pair, pair_send.at[i, c], c)

    for c in range(panels):
        across(0, c).start()
        each(onward, lambda i, c=c: along(i, c).start())
    each(bands - 1, lambda s: send_right(s, layer).start())

    def clear(i):
        for b in range(panels):
            expanded[b, i] = jnp.zeros((tile, tile), jnp.float32)

    each(band_blocks, clear)

    for c in range(panels):

        def forward(i, c=c):
            copy = across(i + 1, c)
            copy.wait_recv()
            copy.start()

        each(onward, forward)

    fetch_right.wait()
    each(bands - 1, lambda s: send_right(s, other(s)).wait_recv())

    def product(d):
        def arrive(h):
            for c in range(panels):
                send_left(owner_at(d * lanes + h, 1 - side), pair, pair_send.at[0, c], c).wait_recv()

        each(lanes, arrive)
        q = xor(own_band, d, bands)
        wanted = right[q, 0:NOTE, :].astype(jnp.float32)
        for p in range(panels):
            for k in range(per_band):
                at = p * per_band + k
                want = wanted[at:at + 1]
                factor = right[q, NOTE + at * tile:NOTE + (at + 1) * tile, :]
                for kk in range(per_band):

                    def choose(o, carry):
                        block, landing = carry
                        owner = q * owners + o
                        notes = left[owner, 0:NOTE, :].astype(jnp.float32)
                        for j in range(panels):
                            t = j * per_band + kk
                            r = jnp.asarray(o * panels + j).astype(jnp.float32)
                            pick = jnp.where(want == r, 1.0, 0.0)
                            tiles = left[owner, NOTE + t * tile:NOTE + (t + 1) * tile, :]
                            block = block + tiles * pick.astype(jnp.bfloat16)
                            landing = landing + notes[t:t + 1] * pick
                        return block, landing

                    carry = jnp.zeros((tile, tile), jnp.bfloat16), jnp.zeros((1, tile), jnp.float32)
                    if owners <= 4:
                        for o in range(owners):
                            carry = choose(o, carry)
                    else:
                        carry = lax.fori_loop(0, owners, choose, carry)
                    block, landing = carry
                    term = jnp.dot(block, factor, preferred_element_type=jnp.float32)

                    def land(b):
                        here = landing == jnp.asarray(b).astype(jnp.float32)
                        expanded[p, b] += jnp.where(here, term, 0.0)

                    if band_blocks <= 4:
                        for b in range(band_blocks):
                            land(b)
                    else:
                        each(band_blocks, land)

    each(bands, product)

    def send_total(s, slot):
        return pltpu.make_async_remote_copy(
            src_ref=totals.at[slot], dst_ref=totals.at[slot], send_sem=total_send.at[s],
            recv_sem=total_recv.at[slot], device_id={"layer": other(s)}, device_id_type=MESH,
        )

    def add(b, sums):
        values = [expanded[p, b] for p in range(panels)]
        return tuple(one + jnp.sum((v * v).reshape(tile // 8, 8, tile), axis=0) for one, v in zip(sums, values))

    sums = lax.fori_loop(0, band_blocks, add, (jnp.zeros((8, tile), jnp.float32),) * panels)
    for p in range(panels):
        totals[layer, p] = sums[p]
    each(bands - 1, lambda s: send_total(s, layer).start())

    row_count = float(panels * cycle * tile)
    fetch_kept.wait()
    fetch_mask.wait()

    def send_out(s, band, p):
        return pltpu.make_async_remote_copy(
            src_ref=stage.at[s, p], dst_ref=out_ref.at[p, band], send_sem=out_send.at[s, p],
            recv_sem=out_recv.at[band, p], device_id={"layer": other(s)}, device_id_type=MESH,
        )

    def keep_own(p):
        return pltpu.make_async_copy(stage.at[bands - 1, p], out_ref.at[p, layer], keep_sem.at[p])

    each(bands - 1, lambda s: send_total(s, other(s)).wait_recv())
    for p in range(panels):
        total = totals[0, p]
        for q in range(1, bands):
            total = total + totals[q, p]
        scale = row_count / jnp.sum(total, axis=0, keepdims=True)
        keep = mask_ref[p, pl.ds(layer, 1), :].astype(jnp.float32)

        def put(s, p=p, scale=scale, keep=keep):
            for j in range(per_layer):
                values = expanded[p, kept_ref[p, 0, other(s) * per_layer + j]]
                stage[s, p, j] = (values * values * scale * keep).astype(jnp.bfloat16)

        def ship(s, p=p, put=put):
            put(s)
            send_out(s, layer, p).start()

        each(bands - 1, ship)
        put(bands - 1)
        keep_own(p).start()

    for p in range(panels):
        each(bands - 1, lambda s, p=p: send_out(s, other(s), p).wait_recv())
        keep_own(p).wait()
    for c in range(panels):
        each(onward, lambda i, c=c: along(i, c).wait_send())
        each(onward + 1, lambda i, c=c: across(i, c).wait_send())
    each(bands - 1, lambda s: send_right(s, layer).wait_send())
    each(bands - 1, lambda s: send_total(s, layer).wait_send())
    for p in range(panels):
        each(bands - 1, lambda s, p=p: send_out(s, layer, p).wait_send())


def solution(mesh):
    cycle, bands = mesh.shape["blk"], mesh.shape["layer"]

    def per_device(tile_values, band_rows, kept_rows, prune_mask):
        panels, _, per_band, tile, _ = tile_values.shape
        per_layer = kept_rows.shape[2] // bands
        band_blocks = panels * cycle // bands
        message = panels * per_band * tile + NOTE
        dma = pltpu.SemaphoreType.DMA
        hbm = pl.BlockSpec(memory_space=pltpu.HBM)
        return pl.pallas_call(
            functools.partial(kernel, cycle, bands, panels, per_band),
            out_shape=jax.ShapeDtypeStruct((panels, bands, per_layer, tile, tile), jnp.bfloat16),
            in_specs=[hbm] * 4,
            out_specs=hbm,
            scratch_shapes=[
                pltpu.VMEM((cycle, message, tile), jnp.bfloat16),
                pltpu.VMEM((bands, message, tile), jnp.bfloat16),
                pltpu.VMEM((panels, band_blocks, tile, tile), jnp.float32),
                pltpu.VMEM((bands, panels, 8, tile), jnp.float32),
                pltpu.VMEM((bands, panels, per_layer, tile, tile), jnp.bfloat16),
                pltpu.SMEM((1, per_band, panels), jnp.int32),
                pltpu.SMEM(kept_rows.shape, jnp.int32),
                pltpu.VMEM(prune_mask.shape, jnp.int32),
                dma((5,)),
                dma((cycle // 2, panels)),
                dma((cycle // 2, panels)),
                dma((bands,)),
                dma((cycle, panels)),
                dma((bands,)),
                dma((bands,)),
                dma((bands,)),
                dma((bands, panels)),
                dma((bands, panels)),
                dma((panels,)),
            ],
            compiler_params=pltpu.CompilerParams(
                collective_id=0, has_side_effects=True, vmem_limit_bytes=63 * 1024 * 1024
            ),
        )(
            tile_values.reshape(panels * per_band * tile, tile),
            band_rows.transpose(1, 2, 0),
            kept_rows,
            prune_mask,
        )

    return jax.shard_map(
        per_device,
        mesh=mesh,
        in_specs=(
            P("blk", "layer", None, None, None),
            P("blk", "layer", None),
            P("blk", "layer", None),
            P("blk", None, None),
        ),
        out_specs=P("blk", None, "layer", None, None),
        check_vma=False,
    )
```

```python
import functools

import jax
import jax.numpy as jnp
from jax import lax
from jax.experimental import pallas as pl
from jax.experimental.pallas import tpu as pltpu
from jax.sharding import PartitionSpec as P

MESH = pl.DeviceIdType.MESH
NOTE = 16


def each(count, body):
    lax.fori_loop(0, count, lambda i, carry: (body(i), carry)[1], 0)


def xor(a, c, count):
    result, bit = 0, 1
    while bit < count:
        result = result + bit * lax.rem(a // bit + c // bit, 2)
        bit *= 2
    return result


def kernel(
    cycle, bands, panels, per_band, tiles_hbm, rows_hbm, kept_hbm, mask_hbm, out_ref,
    left, right, expanded, totals, stage, rows_ref, kept_ref, mask_ref,
    local, up_send, down_send, pair_send, layer_send, left_recv, right_recv,
    total_send, total_recv, out_send, out_recv, keep_sem,
):
    tile = tiles_hbm.shape[1]
    per_layer = out_ref.shape[2]
    body = panels * per_band * tile
    band_blocks = panels * cycle // bands
    owners = band_blocks // panels
    lanes = owners // 2
    me, layer = lax.axis_index("blk"), lax.axis_index("layer")
    side = lax.rem(me, 2)
    pair = me + 1 - 2 * side
    half = cycle // 2
    spot = me // 2
    below, above = spot > 0, spot < half - 1
    own_band, own_lane = me // owners, lax.rem(me // 2, lanes)

    def other(s):
        return lax.rem(layer + 1 + s, bands)

    def owner_at(i, which):
        band = xor(own_band, i // lanes, bands)
        return 2 * (band * lanes + lax.rem(own_lane + lax.rem(i, lanes), lanes)) + which

    fetch_rows = pltpu.make_async_copy(rows_hbm, rows_ref, local.at[0])
    fetch_tiles = pltpu.make_async_copy(tiles_hbm, left.at[me, pl.ds(NOTE, body)], local.at[1])
    fetch_right = pltpu.make_async_copy(tiles_hbm, right.at[layer, pl.ds(NOTE, body)], local.at[2])
    fetch_kept = pltpu.make_async_copy(kept_hbm, kept_ref, local.at[3])
    fetch_mask = pltpu.make_async_copy(mask_hbm, mask_ref, local.at[4])

    barrier = pltpu.get_barrier_semaphore()

    def greet(peer):
        pl.semaphore_signal(barrier, inc=1, device_id=peer, device_id_type=MESH)

    greet({"blk": pair})
    greet({"blk": lax.rem(me + 2, cycle)})
    greet({"blk": lax.rem(me + cycle - 2, cycle)})
    each(bands - 1, lambda s: greet({"layer": other(s)}))
    for fetch in (fetch_rows, fetch_tiles, fetch_right, fetch_kept, fetch_mask):
        fetch.start()

    fetch_rows.wait()
    row_ids = lax.broadcasted_iota(jnp.int32, (NOTE, tile), 0)
    note = jnp.zeros((NOTE, tile), jnp.float32)
    for j in range(panels):
        for k in range(per_band):
            note = jnp.where(row_ids == j * per_band + k, rows_ref[0, k, j].astype(jnp.float32), note)
    note = note.astype(jnp.bfloat16)
    left[me, 0:NOTE, :] = note
    right[layer, 0:NOTE, :] = note
    fetch_tiles.wait()
    pl.semaphore_wait(barrier, 2 + bands)

    part = per_band * tile
    chunks = [(NOTE + c * part if c else 0, part if c else NOTE + part) for c in range(panels)]

    def send_left(slot, target, send_sem, c):
        rows = pl.ds(*chunks[c])
        return pltpu.make_async_remote_copy(
            src_ref=left.at[slot, rows], dst_ref=left.at[slot, rows], send_sem=send_sem,
            recv_sem=left_recv.at[slot, c], device_id={"blk": target}, device_id_type=MESH,
        )

    def send_right(s, band):
        return pltpu.make_async_remote_copy(
            src_ref=left.at[me], dst_ref=right.at[band], send_sem=layer_send.at[s],
            recv_sem=right_recv.at[band], device_id={"layer": other(s)}, device_id_type=MESH,
        )

    def up(t, c):
        return send_left(me - 2 * t, me + 2, up_send.at[t, c], c)

    def down(t, c):
        return send_left(me + 2 * t, me - 2, down_send.at[t, c], c)

    def across(place, c):
        return send_left(2 * place + side, pair, pair_send.at[place, c], c)

    for c in range(panels):
        pl.when(above)(lambda c=c: up(0, c).start())
        pl.when(below)(lambda c=c: down(0, c).start())
        across(spot, c).start()
    each(bands - 1, lambda s: send_right(s, layer).start())

    def clear(i):
        for b in range(panels):
            expanded[b, i] = jnp.zeros((tile, tile), jnp.float32)

    each(band_blocks, clear)

    def pass_on(t):
        for c in range(panels):

            @pl.when(spot > t)
            def _(c=c):
                across(spot - 1 - t, c).wait_recv()
                pl.when(above)(lambda: up(t + 1, c).start())
                across(spot - 1 - t, c).start()

            @pl.when(spot + t < half - 1)
            def _(c=c):
                across(spot + 1 + t, c).wait_recv()
                pl.when(below)(lambda: down(t + 1, c).start())
                across(spot + 1 + t, c).start()

    each(half - 1, pass_on)

    fetch_right.wait()
    each(bands - 1, lambda s: send_right(s, other(s)).wait_recv())

    def product(d):
        def arrive(h):
            for c in range(panels):
                send_left(owner_at(d * lanes + h, 1 - side), pair, pair_send.at[0, c], c).wait_recv()

        each(lanes, arrive)
        q = xor(own_band, d, bands)
        wanted = right[q, 0:NOTE, :].astype(jnp.float32)
        for p in range(panels):
            for k in range(per_band):
                at = p * per_band + k
                want = wanted[at:at + 1]
                factor = right[q, NOTE + at * tile:NOTE + (at + 1) * tile, :]
                for kk in range(per_band):

                    def choose(o, carry):
                        block, landing = carry
                        owner = q * owners + o
                        notes = left[owner, 0:NOTE, :].astype(jnp.float32)
                        for j in range(panels):
                            t = j * per_band + kk
                            r = jnp.asarray(o * panels + j).astype(jnp.float32)
                            pick = jnp.where(want == r, 1.0, 0.0)
                            tiles = left[owner, NOTE + t * tile:NOTE + (t + 1) * tile, :]
                            block = block + tiles * pick.astype(jnp.bfloat16)
                            landing = landing + notes[t:t + 1] * pick
                        return block, landing

                    carry = jnp.zeros((tile, tile), jnp.bfloat16), jnp.zeros((1, tile), jnp.float32)
                    if owners <= 4:
                        for o in range(owners):
                            carry = choose(o, carry)
                    else:
                        carry = lax.fori_loop(0, owners, choose, carry)
                    block, landing = carry
                    term = jnp.dot(block, factor, preferred_element_type=jnp.float32)

                    def land(b):
                        here = landing == jnp.asarray(b).astype(jnp.float32)
                        expanded[p, b] += jnp.where(here, term, 0.0)

                    if band_blocks <= 4:
                        for b in range(band_blocks):
                            land(b)
                    else:
                        each(band_blocks, land)

    each(bands, product)

    def send_total(s, slot):
        return pltpu.make_async_remote_copy(
            src_ref=totals.at[slot], dst_ref=totals.at[slot], send_sem=total_send.at[s],
            recv_sem=total_recv.at[slot], device_id={"layer": other(s)}, device_id_type=MESH,
        )

    def add(b, sums):
        values = [expanded[p, b] for p in range(panels)]
        return tuple(one + jnp.sum((v * v).reshape(tile // 8, 8, tile), axis=0) for one, v in zip(sums, values))

    sums = lax.fori_loop(0, band_blocks, add, (jnp.zeros((8, tile), jnp.float32),) * panels)
    for p in range(panels):
        totals[layer, p] = sums[p]
    each(bands - 1, lambda s: send_total(s, layer).start())

    row_count = float(panels * cycle * tile)
    fetch_kept.wait()
    fetch_mask.wait()

    def send_out(s, band, p):
        return pltpu.make_async_remote_copy(
            src_ref=stage.at[s, p], dst_ref=out_ref.at[p, band], send_sem=out_send.at[s, p],
            recv_sem=out_recv.at[band, p], device_id={"layer": other(s)}, device_id_type=MESH,
        )

    def keep_own(p):
        return pltpu.make_async_copy(stage.at[bands - 1, p], out_ref.at[p, layer], keep_sem.at[p])

    each(bands - 1, lambda s: send_total(s, other(s)).wait_recv())
    for p in range(panels):
        total = totals[0, p]
        for q in range(1, bands):
            total = total + totals[q, p]
        scale = row_count / jnp.sum(total, axis=0, keepdims=True)
        keep = mask_ref[p, pl.ds(layer, 1), :].astype(jnp.float32)

        def put(s, p=p, scale=scale, keep=keep):
            for j in range(per_layer):
                values = expanded[p, kept_ref[p, 0, other(s) * per_layer + j]]
                stage[s, p, j] = (values * values * scale * keep).astype(jnp.bfloat16)

        def ship(s, p=p, put=put):
            put(s)
            send_out(s, layer, p).start()

        each(bands - 1, ship)
        put(bands - 1)
        keep_own(p).start()

    for p in range(panels):
        each(bands - 1, lambda s, p=p: send_out(s, other(s), p).wait_recv())
        keep_own(p).wait()

    def settle(t):
        for c in range(panels):
            across(t, c).wait_send()
            pl.when(above & (t <= spot))(lambda c=c: up(t, c).wait_send())
            pl.when(below & (t < half - spot))(lambda c=c: down(t, c).wait_send())

    each(half, settle)
    each(bands - 1, lambda s: send_right(s, layer).wait_send())
    each(bands - 1, lambda s: send_total(s, layer).wait_send())
    for p in range(panels):
        each(bands - 1, lambda s, p=p: send_out(s, layer, p).wait_send())


def solution(mesh):
    cycle, bands = mesh.shape["blk"], mesh.shape["layer"]

    def per_device(tile_values, band_rows, kept_rows, prune_mask):
        panels, _, per_band, tile, _ = tile_values.shape
        per_layer = kept_rows.shape[2] // bands
        band_blocks = panels * cycle // bands
        message = panels * per_band * tile + NOTE
        dma = pltpu.SemaphoreType.DMA
        hbm = pl.BlockSpec(memory_space=pltpu.HBM)
        return pl.pallas_call(
            functools.partial(kernel, cycle, bands, panels, per_band),
            out_shape=jax.ShapeDtypeStruct((panels, bands, per_layer, tile, tile), jnp.bfloat16),
            in_specs=[hbm] * 4,
            out_specs=hbm,
            scratch_shapes=[
                pltpu.VMEM((cycle, message, tile), jnp.bfloat16),
                pltpu.VMEM((bands, message, tile), jnp.bfloat16),
                pltpu.VMEM((panels, band_blocks, tile, tile), jnp.float32),
                pltpu.VMEM((bands, panels, 8, tile), jnp.float32),
                pltpu.VMEM((bands, panels, per_layer, tile, tile), jnp.bfloat16),
                pltpu.SMEM((1, per_band, panels), jnp.int32),
                pltpu.SMEM(kept_rows.shape, jnp.int32),
                pltpu.VMEM(prune_mask.shape, jnp.int32),
                dma((5,)),
                dma((cycle // 2, panels)),
                dma((cycle // 2, panels)),
                dma((cycle // 2, panels)),
                dma((bands,)),
                dma((cycle, panels)),
                dma((bands,)),
                dma((bands,)),
                dma((bands,)),
                dma((bands, panels)),
                dma((bands, panels)),
                dma((panels,)),
            ],
            compiler_params=pltpu.CompilerParams(
                collective_id=0, has_side_effects=True, vmem_limit_bytes=63 * 1024 * 1024
            ),
        )(
            tile_values.reshape(panels * per_band * tile, tile),
            band_rows.transpose(1, 2, 0),
            kept_rows,
            prune_mask,
        )

    return jax.shard_map(
        per_device,
        mesh=mesh,
        in_specs=(
            P("blk", "layer", None, None, None),
            P("blk", "layer", None),
            P("blk", "layer", None),
            P("blk", None, None),
        ),
        out_specs=P("blk", None, "layer", None, None),
        check_vma=False,
    )
```

```python
import functools

import jax
import jax.numpy as jnp
from jax import lax
from jax.experimental import pallas as pl
from jax.experimental.pallas import tpu as pltpu
from jax.sharding import PartitionSpec as P

MESH = pl.DeviceIdType.MESH
NOTE = 16


def each(count, body):
    lax.fori_loop(0, count, lambda i, carry: (body(i), carry)[1], 0)


def xor(a, c, count):
    result, bit = 0, 1
    while bit < count:
        result = result + bit * lax.rem(a // bit + c // bit, 2)
        bit *= 2
    return result


def kernel(
    cycle, bands, panels, per_band, tiles_hbm, rows_hbm, kept_hbm, mask_hbm, out_ref,
    left, right, expanded, totals, stage, rows_ref, kept_ref, mask_ref,
    local, left_send, layer_send, left_recv, right_recv,
    total_send, total_recv, out_send, out_recv, keep_sem,
):
    tile = tiles_hbm.shape[1]
    per_layer = out_ref.shape[2]
    body = panels * per_band * tile
    band_blocks = panels * cycle // bands
    owners = band_blocks // panels
    me, layer = lax.axis_index("blk"), lax.axis_index("layer")
    own_band = me // owners

    def other(s):
        return lax.rem(layer + 1 + s, bands)

    def target_at(s):
        return lax.rem(me + 1 + s, cycle)

    fetch_rows = pltpu.make_async_copy(rows_hbm, rows_ref, local.at[0])
    fetch_tiles = pltpu.make_async_copy(tiles_hbm, left.at[me, pl.ds(NOTE, body)], local.at[1])
    fetch_right = pltpu.make_async_copy(tiles_hbm, right.at[layer, pl.ds(NOTE, body)], local.at[2])
    fetch_kept = pltpu.make_async_copy(kept_hbm, kept_ref, local.at[3])
    fetch_mask = pltpu.make_async_copy(mask_hbm, mask_ref, local.at[4])

    barrier = pltpu.get_barrier_semaphore()

    def greet(peer):
        pl.semaphore_signal(barrier, inc=1, device_id=peer, device_id_type=MESH)

    each(cycle - 1, lambda s: greet({"blk": target_at(s)}))
    each(bands - 1, lambda s: greet({"layer": other(s)}))
    for fetch in (fetch_rows, fetch_tiles, fetch_right, fetch_kept, fetch_mask):
        fetch.start()

    fetch_rows.wait()
    row_ids = lax.broadcasted_iota(jnp.int32, (NOTE, tile), 0)
    note = jnp.zeros((NOTE, tile), jnp.float32)
    for j in range(panels):
        for k in range(per_band):
            note = jnp.where(row_ids == j * per_band + k, rows_ref[0, k, j].astype(jnp.float32), note)
    note = note.astype(jnp.bfloat16)
    left[me, 0:NOTE, :] = note
    right[layer, 0:NOTE, :] = note
    fetch_tiles.wait()
    pl.semaphore_wait(barrier, cycle + bands - 2)

    def send_left(s, slot):
        return pltpu.make_async_remote_copy(
            src_ref=left.at[slot], dst_ref=left.at[slot], send_sem=left_send.at[s],
            recv_sem=left_recv.at[slot], device_id={"blk": target_at(s)}, device_id_type=MESH,
        )

    def send_right(s, band):
        return pltpu.make_async_remote_copy(
            src_ref=left.at[me], dst_ref=right.at[band], send_sem=layer_send.at[s],
            recv_sem=right_recv.at[band], device_id={"layer": other(s)}, device_id_type=MESH,
        )

    each(cycle - 1, lambda s: send_left(s, me).start())
    each(bands - 1, lambda s: send_right(s, layer).start())

    def clear(i):
        for b in range(panels):
            expanded[b, i] = jnp.zeros((tile, tile), jnp.float32)

    each(band_blocks, clear)

    fetch_right.wait()
    each(bands - 1, lambda s: send_right(s, other(s)).wait_recv())

    def product(d):
        q = xor(own_band, d, bands)

        def arrive(o):
            @pl.when(q * owners + o != me)
            def _():
                send_left(0, q * owners + o).wait_recv()

        each(owners, arrive)
        wanted = right[q, 0:NOTE, :].astype(jnp.float32)
        for p in range(panels):
            for k in range(per_band):
                at = p * per_band + k
                want = wanted[at:at + 1]
                factor = right[q, NOTE + at * tile:NOTE + (at + 1) * tile, :]
                for kk in range(per_band):

                    def choose(o, carry):
                        block, landing = carry
                        owner = q * owners + o
                        notes = left[owner, 0:NOTE, :].astype(jnp.float32)
                        for j in range(panels):
                            t = j * per_band + kk
                            r = jnp.asarray(o * panels + j).astype(jnp.float32)
                            pick = jnp.where(want == r, 1.0, 0.0)
                            tiles = left[owner, NOTE + t * tile:NOTE + (t + 1) * tile, :]
                            block = block + tiles * pick.astype(jnp.bfloat16)
                            landing = landing + notes[t:t + 1] * pick
                        return block, landing

                    carry = jnp.zeros((tile, tile), jnp.bfloat16), jnp.zeros((1, tile), jnp.float32)
                    if owners <= 4:
                        for o in range(owners):
                            carry = choose(o, carry)
                    else:
                        carry = lax.fori_loop(0, owners, choose, carry)
                    block, landing = carry
                    term = jnp.dot(block, factor, preferred_element_type=jnp.float32)

                    def land(b):
                        here = landing == jnp.asarray(b).astype(jnp.float32)
                        expanded[p, b] += jnp.where(here, term, 0.0)

                    if band_blocks <= 4:
                        for b in range(band_blocks):
                            land(b)
                    else:
                        each(band_blocks, land)

    each(bands, product)

    def send_total(s, slot):
        return pltpu.make_async_remote_copy(
            src_ref=totals.at[slot], dst_ref=totals.at[slot], send_sem=total_send.at[s],
            recv_sem=total_recv.at[slot], device_id={"layer": other(s)}, device_id_type=MESH,
        )

    def add(b, sums):
        values = [expanded[p, b] for p in range(panels)]
        return tuple(one + jnp.sum((v * v).reshape(tile // 8, 8, tile), axis=0) for one, v in zip(sums, values))

    sums = lax.fori_loop(0, band_blocks, add, (jnp.zeros((8, tile), jnp.float32),) * panels)
    for p in range(panels):
        totals[layer, p] = sums[p]
    each(bands - 1, lambda s: send_total(s, layer).start())

    row_count = float(panels * cycle * tile)
    fetch_kept.wait()
    fetch_mask.wait()

    def send_out(s, band, p):
        return pltpu.make_async_remote_copy(
            src_ref=stage.at[s, p], dst_ref=out_ref.at[p, band], send_sem=out_send.at[s, p],
            recv_sem=out_recv.at[band, p], device_id={"layer": other(s)}, device_id_type=MESH,
        )

    def keep_own(p):
        return pltpu.make_async_copy(stage.at[bands - 1, p], out_ref.at[p, layer], keep_sem.at[p])

    each(bands - 1, lambda s: send_total(s, other(s)).wait_recv())
    for p in range(panels):
        total = totals[0, p]
        for q in range(1, bands):
            total = total + totals[q, p]
        scale = row_count / jnp.sum(total, axis=0, keepdims=True)
        keep = mask_ref[p, pl.ds(layer, 1), :].astype(jnp.float32)

        def put(s, p=p, scale=scale, keep=keep):
            for j in range(per_layer):
                values = expanded[p, kept_ref[p, 0, other(s) * per_layer + j]]
                stage[s, p, j] = (values * values * scale * keep).astype(jnp.bfloat16)

        def ship(s, p=p, put=put):
            put(s)
            send_out(s, layer, p).start()

        each(bands - 1, ship)
        put(bands - 1)
        keep_own(p).start()

    for p in range(panels):
        each(bands - 1, lambda s, p=p: send_out(s, other(s), p).wait_recv())
        keep_own(p).wait()
    each(cycle - 1, lambda s: send_left(s, me).wait_send())
    each(bands - 1, lambda s: send_right(s, layer).wait_send())
    each(bands - 1, lambda s: send_total(s, layer).wait_send())
    for p in range(panels):
        each(bands - 1, lambda s, p=p: send_out(s, layer, p).wait_send())


def solution(mesh):
    cycle, bands = mesh.shape["blk"], mesh.shape["layer"]

    def per_device(tile_values, band_rows, kept_rows, prune_mask):
        panels, _, per_band, tile, _ = tile_values.shape
        per_layer = kept_rows.shape[2] // bands
        band_blocks = panels * cycle // bands
        message = panels * per_band * tile + NOTE
        dma = pltpu.SemaphoreType.DMA
        hbm = pl.BlockSpec(memory_space=pltpu.HBM)
        return pl.pallas_call(
            functools.partial(kernel, cycle, bands, panels, per_band),
            out_shape=jax.ShapeDtypeStruct((panels, bands, per_layer, tile, tile), jnp.bfloat16),
            in_specs=[hbm] * 4,
            out_specs=hbm,
            scratch_shapes=[
                pltpu.VMEM((cycle, message, tile), jnp.bfloat16),
                pltpu.VMEM((bands, message, tile), jnp.bfloat16),
                pltpu.VMEM((panels, band_blocks, tile, tile), jnp.float32),
                pltpu.VMEM((bands, panels, 8, tile), jnp.float32),
                pltpu.VMEM((bands, panels, per_layer, tile, tile), jnp.bfloat16),
                pltpu.SMEM((1, per_band, panels), jnp.int32),
                pltpu.SMEM(kept_rows.shape, jnp.int32),
                pltpu.VMEM(prune_mask.shape, jnp.int32),
                dma((5,)),
                dma((cycle,)),
                dma((bands,)),
                dma((cycle,)),
                dma((bands,)),
                dma((bands,)),
                dma((bands,)),
                dma((bands, panels)),
                dma((bands, panels)),
                dma((panels,)),
            ],
            compiler_params=pltpu.CompilerParams(
                collective_id=0, has_side_effects=True, vmem_limit_bytes=63 * 1024 * 1024
            ),
        )(
            tile_values.reshape(panels * per_band * tile, tile),
            band_rows.transpose(1, 2, 0),
            kept_rows,
            prune_mask,
        )

    return jax.shard_map(
        per_device,
        mesh=mesh,
        in_specs=(
            P("blk", "layer", None, None, None),
            P("blk", "layer", None),
            P("blk", "layer", None),
            P("blk", None, None),
        ),
        out_specs=P("blk", None, "layer", None, None),
        check_vma=False,
    )
```

```python
import functools

import jax
import jax.numpy as jnp
from jax import lax
from jax.experimental import pallas as pl
from jax.experimental.pallas import tpu as pltpu
from jax.sharding import PartitionSpec as P

MESH = pl.DeviceIdType.MESH
NOTE = 16


def each(count, body):
    lax.fori_loop(0, count, lambda i, carry: (body(i), carry)[1], 0)


def xor(a, c, count):
    result, bit = 0, 1
    while bit < count:
        result = result + bit * lax.rem(a // bit + c // bit, 2)
        bit *= 2
    return result


def kernel(
    cycle, bands, panels, per_band, tiles_hbm, rows_hbm, kept_hbm, mask_hbm, out_ref,
    left, right, expanded, totals, stage, rows_ref, kept_ref, mask_ref,
    local, line_send, pair_send, layer_send, left_recv, right_recv,
    total_send, total_recv, out_send, out_recv, keep_sem,
):
    tile = tiles_hbm.shape[1]
    per_layer = out_ref.shape[2]
    body = panels * per_band * tile
    band_blocks = panels * cycle // bands
    owners = band_blocks // panels
    lanes = owners // 2
    onward = cycle // 2 - 1
    me, layer = lax.axis_index("blk"), lax.axis_index("layer")
    side = lax.rem(me, 2)
    pair = me + 1 - 2 * side
    own_band, own_lane = me // owners, lax.rem(me // 2, lanes)

    def other(s):
        return lax.rem(layer + 1 + s, bands)

    def band_at(i):
        return xor(own_band, lax.rem(bands - i, bands), bands)

    def owner_at(i, which):
        band = band_at(i // lanes)
        return 2 * (band * lanes + lax.rem(own_lane + lax.rem(i, lanes), lanes)) + which

    def target_at(i):
        band = band_at(i // lanes)
        return 2 * (band * lanes + lax.rem(own_lane + lanes - lax.rem(i, lanes), lanes)) + side

    fetch_rows = pltpu.make_async_copy(rows_hbm, rows_ref, local.at[0])
    fetch_tiles = pltpu.make_async_copy(tiles_hbm, left.at[me, pl.ds(NOTE, body)], local.at[1])
    fetch_right = pltpu.make_async_copy(tiles_hbm, right.at[layer, pl.ds(NOTE, body)], local.at[2])
    fetch_kept = pltpu.make_async_copy(kept_hbm, kept_ref, local.at[3])
    fetch_mask = pltpu.make_async_copy(mask_hbm, mask_ref, local.at[4])

    barrier = pltpu.get_barrier_semaphore()

    def greet(peer):
        pl.semaphore_signal(barrier, inc=1, device_id=peer, device_id_type=MESH)

    greet({"blk": pair})
    each(onward, lambda i: greet({"blk": target_at(i + 1)}))
    each(bands - 1, lambda s: greet({"layer": other(s)}))
    for fetch in (fetch_rows, fetch_tiles, fetch_right, fetch_kept, fetch_mask):
        fetch.start()

    fetch_rows.wait()
    row_ids = lax.broadcasted_iota(jnp.int32, (NOTE, tile), 0)
    note = jnp.zeros((NOTE, tile), jnp.float32)
    for j in range(panels):
        for k in range(per_band):
            note = jnp.where(row_ids == j * per_band + k, rows_ref[0, k, j].astype(jnp.float32), note)
    note = note.astype(jnp.bfloat16)
    left[me, 0:NOTE, :] = note
    right[layer, 0:NOTE, :] = note
    fetch_tiles.wait()
    pl.semaphore_wait(barrier, onward + bands)

    part = per_band * tile
    chunks = [(NOTE + c * part if c else 0, part if c else NOTE + part) for c in range(panels)]

    def send_left(slot, target, send_sem, c):
        rows = pl.ds(*chunks[c])
        return pltpu.make_async_remote_copy(
            src_ref=left.at[slot, rows], dst_ref=left.at[slot, rows], send_sem=send_sem,
            recv_sem=left_recv.at[slot, c], device_id={"blk": target}, device_id_type=MESH,
        )

    def send_right(s, band):
        return pltpu.make_async_remote_copy(
            src_ref=left.at[me], dst_ref=right.at[band], send_sem=layer_send.at[s],
            recv_sem=right_recv.at[band], device_id={"layer": other(s)}, device_id_type=MESH,
        )

    def along(i, c):
        return send_left(me, target_at(i + 1), line_send.at[i, c], c)

    def across(i, c):
        return send_left(owner_at(i, side), pair, pair_send.at[i, c], c)

    for c in range(panels):
        across(0, c).start()
        each(onward, lambda i, c=c: along(i, c).start())
    each(bands - 1, lambda s: send_right(s, layer).start())

    def clear(i):
        for b in range(panels):
            expanded[b, i] = jnp.zeros((tile, tile), jnp.float32)

    each(band_blocks, clear)

    for c in range(panels):

        def forward(i, c=c):
            copy = across(i + 1, c)
            copy.wait_recv()
            copy.start()

        each(onward, forward)

    fetch_right.wait()
    each(bands - 1, lambda s: send_right(s, other(s)).wait_recv())

    def product(d):
        def arrive(h):
            for c in range(panels):
                send_left(owner_at(d * lanes + h, 1 - side), pair, pair_send.at[0, c], c).wait_recv()

        each(lanes, arrive)
        q = band_at(d)
        wanted = right[q, 0:NOTE, :].astype(jnp.float32)
        for p in range(panels):
            for k in range(per_band):
                at = p * per_band + k
                want = wanted[at:at + 1]
                factor = right[q, NOTE + at * tile:NOTE + (at + 1) * tile, :]
                for kk in range(per_band):

                    def choose(o, carry):
                        block, landing = carry
                        owner = q * owners + o
                        notes = left[owner, 0:NOTE, :].astype(jnp.float32)
                        for j in range(panels):
                            t = j * per_band + kk
                            r = jnp.asarray(o * panels + j).astype(jnp.float32)
                            pick = jnp.where(want == r, 1.0, 0.0)
                            tiles = left[owner, NOTE + t * tile:NOTE + (t + 1) * tile, :]
                            block = block + tiles * pick.astype(jnp.bfloat16)
                            landing = landing + notes[t:t + 1] * pick
                        return block, landing

                    carry = jnp.zeros((tile, tile), jnp.bfloat16), jnp.zeros((1, tile), jnp.float32)
                    if owners <= 4:
                        for o in range(owners):
                            carry = choose(o, carry)
                    else:
                        carry = lax.fori_loop(0, owners, choose, carry)
                    block, landing = carry
                    term = jnp.dot(block, factor, preferred_element_type=jnp.float32)

                    def land(b):
                        here = landing == jnp.asarray(b).astype(jnp.float32)
                        expanded[p, b] += jnp.where(here, term, 0.0)

                    if band_blocks <= 4:
                        for b in range(band_blocks):
                            land(b)
                    else:
                        each(band_blocks, land)

    each(bands, product)

    def send_total(s, slot):
        return pltpu.make_async_remote_copy(
            src_ref=totals.at[slot], dst_ref=totals.at[slot], send_sem=total_send.at[s],
            recv_sem=total_recv.at[slot], device_id={"layer": other(s)}, device_id_type=MESH,
        )

    def add(b, sums):
        values = [expanded[p, b] for p in range(panels)]
        return tuple(one + jnp.sum((v * v).reshape(tile // 8, 8, tile), axis=0) for one, v in zip(sums, values))

    sums = lax.fori_loop(0, band_blocks, add, (jnp.zeros((8, tile), jnp.float32),) * panels)
    for p in range(panels):
        totals[layer, p] = sums[p]
    each(bands - 1, lambda s: send_total(s, layer).start())

    row_count = float(panels * cycle * tile)
    fetch_kept.wait()
    fetch_mask.wait()

    def send_out(s, band, p):
        return pltpu.make_async_remote_copy(
            src_ref=stage.at[s, p], dst_ref=out_ref.at[p, band], send_sem=out_send.at[s, p],
            recv_sem=out_recv.at[band, p], device_id={"layer": other(s)}, device_id_type=MESH,
        )

    def keep_own(p):
        return pltpu.make_async_copy(stage.at[bands - 1, p], out_ref.at[p, layer], keep_sem.at[p])

    each(bands - 1, lambda s: send_total(s, other(s)).wait_recv())
    for p in range(panels):
        total = totals[0, p]
        for q in range(1, bands):
            total = total + totals[q, p]
        scale = row_count / jnp.sum(total, axis=0, keepdims=True)
        keep = mask_ref[p, pl.ds(layer, 1), :].astype(jnp.float32)

        def put(s, p=p, scale=scale, keep=keep):
            for j in range(per_layer):
                values = expanded[p, kept_ref[p, 0, other(s) * per_layer + j]]
                stage[s, p, j] = (values * values * scale * keep).astype(jnp.bfloat16)

        def ship(s, p=p, put=put):
            put(s)
            send_out(s, layer, p).start()

        each(bands - 1, ship)
        put(bands - 1)
        keep_own(p).start()

    for p in range(panels):
        each(bands - 1, lambda s, p=p: send_out(s, other(s), p).wait_recv())
        keep_own(p).wait()
    for c in range(panels):
        each(onward, lambda i, c=c: along(i, c).wait_send())
        each(onward + 1, lambda i, c=c: across(i, c).wait_send())
    each(bands - 1, lambda s: send_right(s, layer).wait_send())
    each(bands - 1, lambda s: send_total(s, layer).wait_send())
    for p in range(panels):
        each(bands - 1, lambda s, p=p: send_out(s, layer, p).wait_send())


def solution(mesh):
    cycle, bands = mesh.shape["blk"], mesh.shape["layer"]

    def per_device(tile_values, band_rows, kept_rows, prune_mask):
        panels, _, per_band, tile, _ = tile_values.shape
        per_layer = kept_rows.shape[2] // bands
        band_blocks = panels * cycle // bands
        message = panels * per_band * tile + NOTE
        dma = pltpu.SemaphoreType.DMA
        hbm = pl.BlockSpec(memory_space=pltpu.HBM)
        return pl.pallas_call(
            functools.partial(kernel, cycle, bands, panels, per_band),
            out_shape=jax.ShapeDtypeStruct((panels, bands, per_layer, tile, tile), jnp.bfloat16),
            in_specs=[hbm] * 4,
            out_specs=hbm,
            scratch_shapes=[
                pltpu.VMEM((cycle, message, tile), jnp.bfloat16),
                pltpu.VMEM((bands, message, tile), jnp.bfloat16),
                pltpu.VMEM((panels, band_blocks, tile, tile), jnp.float32),
                pltpu.VMEM((bands, panels, 8, tile), jnp.float32),
                pltpu.VMEM((bands, panels, per_layer, tile, tile), jnp.bfloat16),
                pltpu.SMEM((1, per_band, panels), jnp.int32),
                pltpu.SMEM(kept_rows.shape, jnp.int32),
                pltpu.VMEM(prune_mask.shape, jnp.int32),
                dma((5,)),
                dma((cycle // 2, panels)),
                dma((cycle // 2, panels)),
                dma((bands,)),
                dma((cycle, panels)),
                dma((bands,)),
                dma((bands,)),
                dma((bands,)),
                dma((bands, panels)),
                dma((bands, panels)),
                dma((panels,)),
            ],
            compiler_params=pltpu.CompilerParams(
                collective_id=0, has_side_effects=True, vmem_limit_bytes=63 * 1024 * 1024
            ),
        )(
            tile_values.reshape(panels * per_band * tile, tile),
            band_rows.transpose(1, 2, 0),
            kept_rows,
            prune_mask,
        )

    return jax.shard_map(
        per_device,
        mesh=mesh,
        in_specs=(
            P("blk", "layer", None, None, None),
            P("blk", "layer", None),
            P("blk", "layer", None),
            P("blk", None, None),
        ),
        out_specs=P("blk", None, "layer", None, None),
        check_vma=False,
    )
```

```python
import functools

import jax
import jax.numpy as jnp
from jax import lax
from jax.experimental import pallas as pl
from jax.experimental.pallas import tpu as pltpu
from jax.sharding import PartitionSpec as P

MESH = pl.DeviceIdType.MESH
NOTE = 16


def each(count, body):
    lax.fori_loop(0, count, lambda i, carry: (body(i), carry)[1], 0)


def xor(a, c, count):
    result, bit = 0, 1
    while bit < count:
        result = result + bit * lax.rem(a // bit + c // bit, 2)
        bit *= 2
    return result


def kernel(
    cycle, bands, panels, per_band, tiles_hbm, rows_hbm, kept_hbm, mask_hbm, out_ref,
    left, right, expanded, totals, stage, rows_ref, kept_ref, mask_ref,
    local, line_send, direct_send, pair_send, layer_send, left_recv, right_recv,
    total_send, total_recv, out_send, out_recv, keep_sem,
):
    tile = tiles_hbm.shape[1]
    per_layer = out_ref.shape[2]
    body = panels * per_band * tile
    band_blocks = panels * cycle // bands
    owners = band_blocks // panels
    lanes = owners // 2
    onward = cycle // 2 - 1
    me, layer = lax.axis_index("blk"), lax.axis_index("layer")
    side = lax.rem(me, 2)
    pair = me + 1 - 2 * side
    own_band, own_lane = me // owners, lax.rem(me // 2, lanes)

    def other(s):
        return lax.rem(layer + 1 + s, bands)

    def owner_at(i, which):
        band = xor(own_band, i // lanes, bands)
        return 2 * (band * lanes + lax.rem(own_lane + lax.rem(i, lanes), lanes)) + which

    def target_at(i):
        band = xor(own_band, i // lanes, bands)
        return 2 * (band * lanes + lax.rem(own_lane + lanes - lax.rem(i, lanes), lanes)) + side

    fetch_rows = pltpu.make_async_copy(rows_hbm, rows_ref, local.at[0])
    fetch_tiles = pltpu.make_async_copy(tiles_hbm, left.at[me, pl.ds(NOTE, body)], local.at[1])
    fetch_right = pltpu.make_async_copy(tiles_hbm, right.at[layer, pl.ds(NOTE, body)], local.at[2])
    fetch_kept = pltpu.make_async_copy(kept_hbm, kept_ref, local.at[3])
    fetch_mask = pltpu.make_async_copy(mask_hbm, mask_ref, local.at[4])

    barrier = pltpu.get_barrier_semaphore()

    def greet(peer):
        pl.semaphore_signal(barrier, inc=1, device_id=peer, device_id_type=MESH)

    greet({"blk": pair})
    each(onward, lambda i: greet({"blk": target_at(i + 1)}))
    each(onward, lambda i: greet({"blk": target_at(i + 1) + pair - me}))
    each(bands - 1, lambda s: greet({"layer": other(s)}))
    for fetch in (fetch_rows, fetch_tiles, fetch_right, fetch_kept, fetch_mask):
        fetch.start()

    fetch_rows.wait()
    row_ids = lax.broadcasted_iota(jnp.int32, (NOTE, tile), 0)
    note = jnp.zeros((NOTE, tile), jnp.float32)
    for j in range(panels):
        for k in range(per_band):
            note = jnp.where(row_ids == j * per_band + k, rows_ref[0, k, j].astype(jnp.float32), note)
    note = note.astype(jnp.bfloat16)
    left[me, 0:NOTE, :] = note
    right[layer, 0:NOTE, :] = note
    fetch_tiles.wait()
    pl.semaphore_wait(barrier, 2 * onward + bands)

    part = per_band * tile
    chunks = [(NOTE + c * part if c else 0, part if c else NOTE + part) for c in range(panels)]

    def send_left(slot, target, send_sem, c):
        rows = pl.ds(*chunks[c])
        return pltpu.make_async_remote_copy(
            src_ref=left.at[slot, rows], dst_ref=left.at[slot, rows], send_sem=send_sem,
            recv_sem=left_recv.at[slot, c], device_id={"blk": target}, device_id_type=MESH,
        )

    def send_right(s, band):
        return pltpu.make_async_remote_copy(
            src_ref=left.at[me], dst_ref=right.at[band], send_sem=layer_send.at[s],
            recv_sem=right_recv.at[band], device_id={"layer": other(s)}, device_id_type=MESH,
        )

    def along(i, c):
        return send_left(me, target_at(i + 1), line_send.at[i, c], c)

    def direct(i, c):
        return send_left(me, target_at(i + 1) + pair - me, direct_send.at[i, c], c)

    def across(i, c):
        return send_left(owner_at(i, side), pair, pair_send.at[i, c], c)

    for c in range(panels):
        across(0, c).start()
        each(onward, lambda i, c=c: along(i, c).start())
        if c:
            each(onward, lambda i, c=c: direct(i, c).start())
    each(bands - 1, lambda s: send_right(s, layer).start())

    def clear(i):
        for b in range(panels):
            expanded[b, i] = jnp.zeros((tile, tile), jnp.float32)

    each(band_blocks, clear)

    def forward(i):
        copy = across(i + 1, 0)
        copy.wait_recv()
        copy.start()

    each(onward, forward)

    fetch_right.wait()
    each(bands - 1, lambda s: send_right(s, other(s)).wait_recv())

    def product(d):
        def arrive(h):
            for c in range(panels):
                send_left(owner_at(d * lanes + h, 1 - side), pair, pair_send.at[0, c], c).wait_recv()
            for c in range(1, panels):
                source = owner_at(d * lanes + h, side)

                @pl.when(source != me)
                def _(c=c, source=source):
                    send_left(source, pair, pair_send.at[0, c], c).wait_recv()

        each(lanes, arrive)
        q = xor(own_band, d, bands)
        wanted = right[q, 0:NOTE, :].astype(jnp.float32)
        for p in range(panels):
            for k in range(per_band):
                at = p * per_band + k
                want = wanted[at:at + 1]
                factor = right[q, NOTE + at * tile:NOTE + (at + 1) * tile, :]
                for kk in range(per_band):

                    def choose(o, carry):
                        block, landing = carry
                        owner = q * owners + o
                        notes = left[owner, 0:NOTE, :].astype(jnp.float32)
                        for j in range(panels):
                            t = j * per_band + kk
                            r = jnp.asarray(o * panels + j).astype(jnp.float32)
                            pick = jnp.where(want == r, 1.0, 0.0)
                            tiles = left[owner, NOTE + t * tile:NOTE + (t + 1) * tile, :]
                            block = block + tiles * pick.astype(jnp.bfloat16)
                            landing = landing + notes[t:t + 1] * pick
                        return block, landing

                    carry = jnp.zeros((tile, tile), jnp.bfloat16), jnp.zeros((1, tile), jnp.float32)
                    if owners <= 4:
                        for o in range(owners):
                            carry = choose(o, carry)
                    else:
                        carry = lax.fori_loop(0, owners, choose, carry)
                    block, landing = carry
                    term = jnp.dot(block, factor, preferred_element_type=jnp.float32)

                    def land(b):
                        here = landing == jnp.asarray(b).astype(jnp.float32)
                        expanded[p, b] += jnp.where(here, term, 0.0)

                    if band_blocks <= 4:
                        for b in range(band_blocks):
                            land(b)
                    else:
                        each(band_blocks, land)

    each(bands, product)

    def send_total(s, slot):
        return pltpu.make_async_remote_copy(
            src_ref=totals.at[slot], dst_ref=totals.at[slot], send_sem=total_send.at[s],
            recv_sem=total_recv.at[slot], device_id={"layer": other(s)}, device_id_type=MESH,
        )

    def add(b, sums):
        values = [expanded[p, b] for p in range(panels)]
        return tuple(one + jnp.sum((v * v).reshape(tile // 8, 8, tile), axis=0) for one, v in zip(sums, values))

    sums = lax.fori_loop(0, band_blocks, add, (jnp.zeros((8, tile), jnp.float32),) * panels)
    for p in range(panels):
        totals[layer, p] = sums[p]
    each(bands - 1, lambda s: send_total(s, layer).start())

    row_count = float(panels * cycle * tile)
    fetch_kept.wait()
    fetch_mask.wait()

    def send_out(s, band, p):
        return pltpu.make_async_remote_copy(
            src_ref=stage.at[s, p], dst_ref=out_ref.at[p, band], send_sem=out_send.at[s, p],
            recv_sem=out_recv.at[band, p], device_id={"layer": other(s)}, device_id_type=MESH,
        )

    def keep_own(p):
        return pltpu.make_async_copy(stage.at[bands - 1, p], out_ref.at[p, layer], keep_sem.at[p])

    each(bands - 1, lambda s: send_total(s, other(s)).wait_recv())
    for p in range(panels):
        total = totals[0, p]
        for q in range(1, bands):
            total = total + totals[q, p]
        scale = row_count / jnp.sum(total, axis=0, keepdims=True)
        keep = mask_ref[p, pl.ds(layer, 1), :].astype(jnp.float32)

        def put(s, p=p, scale=scale, keep=keep):
            for j in range(per_layer):
                values = expanded[p, kept_ref[p, 0, other(s) * per_layer + j]]
                stage[s, p, j] = (values * values * scale * keep).astype(jnp.bfloat16)

        def ship(s, p=p, put=put):
            put(s)
            send_out(s, layer, p).start()

        each(bands - 1, ship)
        put(bands - 1)
        keep_own(p).start()

    for p in range(panels):
        each(bands - 1, lambda s, p=p: send_out(s, other(s), p).wait_recv())
        keep_own(p).wait()
    for c in range(panels):
        each(onward, lambda i, c=c: along(i, c).wait_send())
        each(1 if c else onward + 1, lambda i, c=c: across(i, c).wait_send())
        if c:
            each(onward, lambda i, c=c: direct(i, c).wait_send())
    each(bands - 1, lambda s: send_right(s, layer).wait_send())
    each(bands - 1, lambda s: send_total(s, layer).wait_send())
    for p in range(panels):
        each(bands - 1, lambda s, p=p: send_out(s, layer, p).wait_send())


def solution(mesh):
    cycle, bands = mesh.shape["blk"], mesh.shape["layer"]

    def per_device(tile_values, band_rows, kept_rows, prune_mask):
        panels, _, per_band, tile, _ = tile_values.shape
        per_layer = kept_rows.shape[2] // bands
        band_blocks = panels * cycle // bands
        message = panels * per_band * tile + NOTE
        dma = pltpu.SemaphoreType.DMA
        hbm = pl.BlockSpec(memory_space=pltpu.HBM)
        return pl.pallas_call(
            functools.partial(kernel, cycle, bands, panels, per_band),
            out_shape=jax.ShapeDtypeStruct((panels, bands, per_layer, tile, tile), jnp.bfloat16),
            in_specs=[hbm] * 4,
            out_specs=hbm,
            scratch_shapes=[
                pltpu.VMEM((cycle, message, tile), jnp.bfloat16),
                pltpu.VMEM((bands, message, tile), jnp.bfloat16),
                pltpu.VMEM((panels, band_blocks, tile, tile), jnp.float32),
                pltpu.VMEM((bands, panels, 8, tile), jnp.float32),
                pltpu.VMEM((bands, panels, per_layer, tile, tile), jnp.bfloat16),
                pltpu.SMEM((1, per_band, panels), jnp.int32),
                pltpu.SMEM(kept_rows.shape, jnp.int32),
                pltpu.VMEM(prune_mask.shape, jnp.int32),
                dma((5,)),
                dma((cycle // 2, panels)),
                dma((cycle // 2, panels)),
                dma((cycle // 2, panels)),
                dma((bands,)),
                dma((cycle, panels)),
                dma((bands,)),
                dma((bands,)),
                dma((bands,)),
                dma((bands, panels)),
                dma((bands, panels)),
                dma((panels,)),
            ],
            compiler_params=pltpu.CompilerParams(
                collective_id=0, has_side_effects=True, vmem_limit_bytes=63 * 1024 * 1024
            ),
        )(
            tile_values.reshape(panels * per_band * tile, tile),
            band_rows.transpose(1, 2, 0),
            kept_rows,
            prune_mask,
        )

    return jax.shard_map(
        per_device,
        mesh=mesh,
        in_specs=(
            P("blk", "layer", None, None, None),
            P("blk", "layer", None),
            P("blk", "layer", None),
            P("blk", None, None),
        ),
        out_specs=P("blk", None, "layer", None, None),
        check_vma=False,
    )
```

```python
import functools

import jax
import jax.numpy as jnp
from jax import lax
from jax.experimental import pallas as pl
from jax.experimental.pallas import tpu as pltpu
from jax.sharding import PartitionSpec as P

MESH = pl.DeviceIdType.MESH
NOTE = 16


def each(count, body):
    lax.fori_loop(0, count, lambda i, carry: (body(i), carry)[1], 0)


def xor(a, c, count):
    result, bit = 0, 1
    while bit < count:
        result = result + bit * lax.rem(a // bit + c // bit, 2)
        bit *= 2
    return result


def kernel(
    cycle, bands, panels, per_band, tiles_hbm, rows_hbm, kept_hbm, mask_hbm, out_ref,
    left, right, expanded, totals, stage, rows_ref, kept_ref, mask_ref,
    local, line_send, pair_send, layer_send, left_recv, right_recv,
    total_send, total_recv, out_send, out_recv, keep_sem,
):
    tile = tiles_hbm.shape[1]
    per_layer = out_ref.shape[2]
    body = panels * per_band * tile
    band_blocks = panels * cycle // bands
    owners = band_blocks // panels
    lanes = owners // 2
    onward = cycle // 2 - 1
    me, layer = lax.axis_index("blk"), lax.axis_index("layer")
    side = lax.rem(me, 2)
    pair = me + 1 - 2 * side
    own_band, own_lane = me // owners, lax.rem(me // 2, lanes)

    def other(s):
        return lax.rem(layer + 1 + s, bands)

    def owner_at(i, which):
        band = xor(own_band, i // lanes, bands)
        return 2 * (band * lanes + lax.rem(own_lane + lax.rem(i, lanes), lanes)) + which

    def target_at(i):
        band = xor(own_band, i // lanes, bands)
        return 2 * (band * lanes + lax.rem(own_lane + lanes - lax.rem(i, lanes), lanes)) + side

    fetch_rows = pltpu.make_async_copy(rows_hbm, rows_ref, local.at[0])
    fetch_tiles = pltpu.make_async_copy(tiles_hbm, left.at[me, pl.ds(NOTE, body)], local.at[1])
    fetch_right = pltpu.make_async_copy(tiles_hbm, right.at[layer, pl.ds(NOTE, body)], local.at[2])
    fetch_kept = pltpu.make_async_copy(kept_hbm, kept_ref, local.at[3])
    fetch_mask = pltpu.make_async_copy(mask_hbm, mask_ref, local.at[4])

    barrier = pltpu.get_barrier_semaphore()

    def greet(peer):
        pl.semaphore_signal(barrier, inc=1, device_id=peer, device_id_type=MESH)

    greet({"blk": pair})
    each(onward, lambda i: greet({"blk": target_at(i + 1)}))
    each(bands - 1, lambda s: greet({"layer": other(s)}))
    for fetch in (fetch_rows, fetch_tiles, fetch_right, fetch_kept, fetch_mask):
        fetch.start()

    fetch_rows.wait()
    row_ids = lax.broadcasted_iota(jnp.int32, (NOTE, tile), 0)
    note = jnp.zeros((NOTE, tile), jnp.float32)
    for j in range(panels):
        for k in range(per_band):
            note = jnp.where(row_ids == j * per_band + k, rows_ref[0, k, j].astype(jnp.float32), note)
    note = note.astype(jnp.bfloat16)
    left[me, 0:NOTE, :] = note
    right[layer, 0:NOTE, :] = note
    fetch_tiles.wait()
    pl.semaphore_wait(barrier, onward + bands)

    part = per_band * tile
    chunks = [(NOTE + c * part if c else 0, part if c else NOTE + part) for c in range(panels)]

    def send_left(slot, target, send_sem, c):
        rows = pl.ds(*chunks[c])
        return pltpu.make_async_remote_copy(
            src_ref=left.at[slot, rows], dst_ref=left.at[slot, rows], send_sem=send_sem,
            recv_sem=left_recv.at[slot, c], device_id={"blk": target}, device_id_type=MESH,
        )

    def send_right(s, band):
        return pltpu.make_async_remote_copy(
            src_ref=left.at[me], dst_ref=right.at[band], send_sem=layer_send.at[s],
            recv_sem=right_recv.at[band], device_id={"layer": other(s)}, device_id_type=MESH,
        )

    def along(i, c):
        return send_left(me, target_at(i + 1), line_send.at[i, c], c)

    def across(i, c):
        return send_left(owner_at(i, side), pair, pair_send.at[i, c], c)

    for c in range(panels):
        across(0, c).start()
        each(onward, lambda i, c=c: along(i, c).start())
    each(bands - 1, lambda s: send_right(s, layer).start())

    def clear(i):
        for b in range(panels):
            expanded[b, i] = jnp.zeros((tile, tile), jnp.float32)

    each(band_blocks, clear)

    for c in range(panels):

        def forward(i, c=c):
            copy = across(i + 1, c)
            copy.wait_recv()
            copy.start()

        each(onward, forward)

    fetch_right.wait()
    each(bands - 1, lambda s: send_right(s, other(s)).wait_recv())

    def product(d):
        def arrive(h):
            for c in range(panels):
                send_left(owner_at(d * lanes + h, 1 - side), pair, pair_send.at[0, c], c).wait_recv()

        each(lanes, arrive)
        q = xor(own_band, d, bands)
        wanted = right[q, 0:NOTE, :].astype(jnp.float32)
        for p in range(panels):
            for k in range(per_band):
                at = p * per_band + k
                want = wanted[at:at + 1]
                factor = right[q, NOTE + at * tile:NOTE + (at + 1) * tile, :]
                for kk in range(per_band):

                    def choose(o, carry):
                        block, landing = carry
                        owner = q * owners + o
                        notes = left[owner, 0:NOTE, :].astype(jnp.float32)
                        for j in range(panels):
                            t = j * per_band + kk
                            r = jnp.asarray(o * panels + j).astype(jnp.float32)
                            pick = jnp.where(want == r, 1.0, 0.0)
                            tiles = left[owner, NOTE + t * tile:NOTE + (t + 1) * tile, :]
                            block = block + tiles * pick.astype(jnp.bfloat16)
                            landing = landing + notes[t:t + 1] * pick
                        return block, landing

                    carry = jnp.zeros((tile, tile), jnp.bfloat16), jnp.zeros((1, tile), jnp.float32)
                    if owners <= 4:
                        for o in range(owners):
                            carry = choose(o, carry)
                    else:
                        carry = lax.fori_loop(0, owners, choose, carry)
                    block, landing = carry
                    term = jnp.dot(block, factor, preferred_element_type=jnp.float32)

                    def land(b):
                        here = landing == jnp.asarray(b).astype(jnp.float32)
                        expanded[p, b] += jnp.where(here, term, 0.0)

                    if band_blocks <= 4:
                        for b in range(band_blocks):
                            land(b)
                    else:
                        each(band_blocks, land)

    each(bands, product)

    def send_total(s, slot):
        return pltpu.make_async_remote_copy(
            src_ref=totals.at[slot], dst_ref=totals.at[slot], send_sem=total_send.at[s],
            recv_sem=total_recv.at[slot], device_id={"layer": other(s)}, device_id_type=MESH,
        )

    def add(b, sums):
        values = [expanded[p, b] for p in range(panels)]
        return tuple(one + jnp.sum((v * v).reshape(tile // 8, 8, tile), axis=0) for one, v in zip(sums, values))

    sums = lax.fori_loop(0, band_blocks, add, (jnp.zeros((8, tile), jnp.float32),) * panels)
    for p in range(panels):
        totals[layer, p] = sums[p]
    each(bands - 1, lambda s: send_total(s, layer).start())

    row_count = float(panels * cycle * tile)
    fetch_kept.wait()
    fetch_mask.wait()

    def send_out(s, band, p):
        return pltpu.make_async_remote_copy(
            src_ref=stage.at[s, p], dst_ref=out_ref.at[p, band], send_sem=out_send.at[s, p],
            recv_sem=out_recv.at[band, p], device_id={"layer": other(s)}, device_id_type=MESH,
        )

    def keep_own(p):
        return pltpu.make_async_copy(stage.at[bands - 1, p], out_ref.at[p, layer], keep_sem.at[p])

    each(bands - 1, lambda s: send_total(s, other(s)).wait_recv())
    for p in range(panels):
        total = totals[0, p]
        for q in range(1, bands):
            total = total + totals[q, p]
        scale = row_count / jnp.sum(total, axis=0, keepdims=True)
        keep = mask_ref[p, pl.ds(layer, 1), :].astype(jnp.float32)

        def put(s, p=p, scale=scale, keep=keep):
            for j in range(per_layer):
                values = expanded[p, kept_ref[p, 0, other(s) * per_layer + j]]
                stage[s, p, j] = (values * values * scale * keep).astype(jnp.bfloat16)

        def ship(s, p=p, put=put):
            put(s)
            send_out(s, layer, p).start()

        each(bands - 1, ship)
        put(bands - 1)
        keep_own(p).start()

    for p in range(panels):
        each(bands - 1, lambda s, p=p: send_out(s, other(s), p).wait_recv())
        keep_own(p).wait()
    for c in range(panels):
        each(onward, lambda i, c=c: along(i, c).wait_send())
        each(onward + 1, lambda i, c=c: across(i, c).wait_send())
    each(bands - 1, lambda s: send_right(s, layer).wait_send())
    each(bands - 1, lambda s: send_total(s, layer).wait_send())
    for p in range(panels):
        each(bands - 1, lambda s, p=p: send_out(s, layer, p).wait_send())


def solution(mesh):
    cycle, bands = mesh.shape["blk"], mesh.shape["layer"]

    def per_device(tile_values, band_rows, kept_rows, prune_mask):
        panels, _, per_band, tile, _ = tile_values.shape
        per_layer = kept_rows.shape[2] // bands
        band_blocks = panels * cycle // bands
        message = panels * per_band * tile + NOTE
        dma = pltpu.SemaphoreType.DMA
        hbm = pl.BlockSpec(memory_space=pltpu.HBM)
        return pl.pallas_call(
            functools.partial(kernel, cycle, bands, panels, per_band),
            out_shape=jax.ShapeDtypeStruct((panels, bands, per_layer, tile, tile), jnp.bfloat16),
            in_specs=[hbm] * 4,
            out_specs=pl.BlockSpec(memory_space=pltpu.VMEM),
            scratch_shapes=[
                pltpu.VMEM((cycle, message, tile), jnp.bfloat16),
                pltpu.VMEM((bands, message, tile), jnp.bfloat16),
                pltpu.VMEM((panels, band_blocks, tile, tile), jnp.float32),
                pltpu.VMEM((bands, panels, 8, tile), jnp.float32),
                pltpu.VMEM((bands, panels, per_layer, tile, tile), jnp.bfloat16),
                pltpu.SMEM((1, per_band, panels), jnp.int32),
                pltpu.SMEM(kept_rows.shape, jnp.int32),
                pltpu.VMEM(prune_mask.shape, jnp.int32),
                dma((5,)),
                dma((cycle // 2, panels)),
                dma((cycle // 2, panels)),
                dma((bands,)),
                dma((cycle, panels)),
                dma((bands,)),
                dma((bands,)),
                dma((bands,)),
                dma((bands, panels)),
                dma((bands, panels)),
                dma((panels,)),
            ],
            compiler_params=pltpu.CompilerParams(
                collective_id=0, has_side_effects=True, vmem_limit_bytes=32 * 1024 * 1024
            ),
        )(
            tile_values.reshape(panels * per_band * tile, tile),
            band_rows.transpose(1, 2, 0),
            kept_rows,
            prune_mask,
        )

    return jax.shard_map(
        per_device,
        mesh=mesh,
        in_specs=(
            P("blk", "layer", None, None, None),
            P("blk", "layer", None),
            P("blk", "layer", None),
            P("blk", None, None),
        ),
        out_specs=P("blk", None, "layer", None, None),
        check_vma=False,
    )
```

```python
import functools

import jax
import jax.numpy as jnp
from jax import lax
from jax.experimental import pallas as pl
from jax.experimental.pallas import tpu as pltpu
from jax.sharding import PartitionSpec as P

MESH = pl.DeviceIdType.MESH
NOTE = 16


def each(count, body):
    lax.fori_loop(0, count, lambda i, carry: (body(i), carry)[1], 0)


def xor(a, c, count):
    result, bit = 0, 1
    while bit < count:
        result = result + bit * lax.rem(a // bit + c // bit, 2)
        bit *= 2
    return result


def kernel(
    cycle, bands, panels, per_band, tiles_hbm, rows_hbm, kept_hbm, mask_hbm, out_ref,
    left, right, expanded, totals, stage, rows_ref, kept_ref, mask_ref,
    local, line_send, pair_send, layer_send, left_recv, right_recv,
    total_send, total_recv, out_send, out_recv, keep_sem,
):
    tile = tiles_hbm.shape[1]
    per_layer = out_ref.shape[2]
    body = panels * per_band * tile
    band_blocks = panels * cycle // bands
    owners = band_blocks // panels
    lanes = owners // 2
    onward = cycle // 2 - 1
    me, layer = lax.axis_index("blk"), lax.axis_index("layer")
    side = lax.rem(me, 2)
    pair = me + 1 - 2 * side
    own_band, own_lane = me // owners, lax.rem(me // 2, lanes)

    def other(s):
        return lax.rem(layer + 1 + s, bands)

    def owner_at(i, which):
        band = xor(own_band, i // lanes, bands)
        return 2 * (band * lanes + lax.rem(own_lane + lax.rem(i, lanes), lanes)) + which

    def target_at(i):
        band = xor(own_band, i // lanes, bands)
        return 2 * (band * lanes + lax.rem(own_lane + lanes - lax.rem(i, lanes), lanes)) + side

    fetch_rows = pltpu.make_async_copy(rows_hbm, rows_ref, local.at[0])
    fetch_tiles = pltpu.make_async_copy(tiles_hbm, left.at[me, pl.ds(NOTE, body)], local.at[1])
    fetch_right = pltpu.make_async_copy(tiles_hbm, right.at[layer, pl.ds(NOTE, body)], local.at[2])
    fetch_kept = pltpu.make_async_copy(kept_hbm, kept_ref, local.at[3])
    fetch_mask = pltpu.make_async_copy(mask_hbm, mask_ref, local.at[4])

    barrier = pltpu.get_barrier_semaphore()

    def greet(peer):
        pl.semaphore_signal(barrier, inc=1, device_id=peer, device_id_type=MESH)

    greet({"blk": pair})
    each(onward, lambda i: greet({"blk": target_at(i + 1)}))
    each(bands - 1, lambda s: greet({"layer": other(s)}))
    for fetch in (fetch_rows, fetch_tiles, fetch_right, fetch_kept, fetch_mask):
        fetch.start()

    fetch_rows.wait()
    row_ids = lax.broadcasted_iota(jnp.int32, (NOTE, tile), 0)
    note = jnp.zeros((NOTE, tile), jnp.float32)
    for j in range(panels):
        for k in range(per_band):
            note = jnp.where(row_ids == j * per_band + k, rows_ref[0, k, j].astype(jnp.float32), note)
    note = note.astype(jnp.bfloat16)
    left[me, 0:NOTE, :] = note
    right[layer, 0:NOTE, :] = note
    fetch_tiles.wait()
    pl.semaphore_wait(barrier, onward + bands)

    chunks = [(0, NOTE + body)]

    def send_left(slot, target, send_sem, c):
        rows = pl.ds(*chunks[c])
        return pltpu.make_async_remote_copy(
            src_ref=left.at[slot, rows], dst_ref=left.at[slot, rows], send_sem=send_sem,
            recv_sem=left_recv.at[slot, c], device_id={"blk": target}, device_id_type=MESH,
        )

    def send_right(s, band):
        return pltpu.make_async_remote_copy(
            src_ref=left.at[me], dst_ref=right.at[band], send_sem=layer_send.at[s],
            recv_sem=right_recv.at[band], device_id={"layer": other(s)}, device_id_type=MESH,
        )

    def along(i, c):
        return send_left(me, target_at(i + 1), line_send.at[i, c], c)

    def across(i, c):
        return send_left(owner_at(i, side), pair, pair_send.at[i, c], c)

    for c in range(len(chunks)):
        across(0, c).start()
        each(onward, lambda i, c=c: along(i, c).start())
    each(bands - 1, lambda s: send_right(s, layer).start())

    def clear(i):
        for b in range(panels):
            expanded[b, i] = jnp.zeros((tile, tile), jnp.float32)

    each(band_blocks, clear)

    for c in range(len(chunks)):

        def forward(i, c=c):
            copy = across(i + 1, c)
            copy.wait_recv()
            copy.start()

        each(onward, forward)

    fetch_right.wait()
    each(bands - 1, lambda s: send_right(s, other(s)).wait_recv())

    def product(d):
        def arrive(h):
            for c in range(len(chunks)):
                send_left(owner_at(d * lanes + h, 1 - side), pair, pair_send.at[0, c], c).wait_recv()

        each(lanes, arrive)
        q = xor(own_band, d, bands)
        wanted = right[q, 0:NOTE, :].astype(jnp.float32)
        for p in range(panels):
            for k in range(per_band):
                at = p * per_band + k
                want = wanted[at:at + 1]
                factor = right[q, NOTE + at * tile:NOTE + (at + 1) * tile, :]
                for kk in range(per_band):

                    def choose(o, carry):
                        block, landing = carry
                        owner = q * owners + o
                        notes = left[owner, 0:NOTE, :].astype(jnp.float32)
                        for j in range(panels):
                            t = j * per_band + kk
                            r = jnp.asarray(o * panels + j).astype(jnp.float32)
                            pick = jnp.where(want == r, 1.0, 0.0)
                            tiles = left[owner, NOTE + t * tile:NOTE + (t + 1) * tile, :]
                            block = block + tiles * pick.astype(jnp.bfloat16)
                            landing = landing + notes[t:t + 1] * pick
                        return block, landing

                    carry = jnp.zeros((tile, tile), jnp.bfloat16), jnp.zeros((1, tile), jnp.float32)
                    if owners <= 4:
                        for o in range(owners):
                            carry = choose(o, carry)
                    else:
                        carry = lax.fori_loop(0, owners, choose, carry)
                    block, landing = carry
                    term = jnp.dot(block, factor, preferred_element_type=jnp.float32)

                    def land(b):
                        here = landing == jnp.asarray(b).astype(jnp.float32)
                        expanded[p, b] += jnp.where(here, term, 0.0)

                    if band_blocks <= 4:
                        for b in range(band_blocks):
                            land(b)
                    else:
                        each(band_blocks, land)

    each(bands, product)

    def send_total(s, slot):
        return pltpu.make_async_remote_copy(
            src_ref=totals.at[slot], dst_ref=totals.at[slot], send_sem=total_send.at[s],
            recv_sem=total_recv.at[slot], device_id={"layer": other(s)}, device_id_type=MESH,
        )

    def add(b, sums):
        values = [expanded[p, b] for p in range(panels)]
        return tuple(one + jnp.sum((v * v).reshape(tile // 8, 8, tile), axis=0) for one, v in zip(sums, values))

    sums = lax.fori_loop(0, band_blocks, add, (jnp.zeros((8, tile), jnp.float32),) * panels)
    for p in range(panels):
        totals[layer, p] = sums[p]
    each(bands - 1, lambda s: send_total(s, layer).start())

    row_count = float(panels * cycle * tile)
    fetch_kept.wait()
    fetch_mask.wait()

    def send_out(s, band, p):
        return pltpu.make_async_remote_copy(
            src_ref=stage.at[s, p], dst_ref=out_ref.at[p, band], send_sem=out_send.at[s, p],
            recv_sem=out_recv.at[band, p], device_id={"layer": other(s)}, device_id_type=MESH,
        )

    def keep_own(p):
        return pltpu.make_async_copy(stage.at[bands - 1, p], out_ref.at[p, layer], keep_sem.at[p])

    each(bands - 1, lambda s: send_total(s, other(s)).wait_recv())
    for p in range(panels):
        total = totals[0, p]
        for q in range(1, bands):
            total = total + totals[q, p]
        scale = row_count / jnp.sum(total, axis=0, keepdims=True)
        keep = mask_ref[p, pl.ds(layer, 1), :].astype(jnp.float32)

        def put(s, p=p, scale=scale, keep=keep):
            for j in range(per_layer):
                values = expanded[p, kept_ref[p, 0, other(s) * per_layer + j]]
                stage[s, p, j] = (values * values * scale * keep).astype(jnp.bfloat16)

        def ship(s, p=p, put=put):
            put(s)
            send_out(s, layer, p).start()

        each(bands - 1, ship)
        put(bands - 1)
        keep_own(p).start()

    for p in range(panels):
        each(bands - 1, lambda s, p=p: send_out(s, other(s), p).wait_recv())
        keep_own(p).wait()
    for c in range(len(chunks)):
        each(onward, lambda i, c=c: along(i, c).wait_send())
        each(onward + 1, lambda i, c=c: across(i, c).wait_send())
    each(bands - 1, lambda s: send_right(s, layer).wait_send())
    each(bands - 1, lambda s: send_total(s, layer).wait_send())
    for p in range(panels):
        each(bands - 1, lambda s, p=p: send_out(s, layer, p).wait_send())


def solution(mesh):
    cycle, bands = mesh.shape["blk"], mesh.shape["layer"]

    def per_device(tile_values, band_rows, kept_rows, prune_mask):
        panels, _, per_band, tile, _ = tile_values.shape
        per_layer = kept_rows.shape[2] // bands
        band_blocks = panels * cycle // bands
        message = panels * per_band * tile + NOTE
        dma = pltpu.SemaphoreType.DMA
        hbm = pl.BlockSpec(memory_space=pltpu.HBM)
        return pl.pallas_call(
            functools.partial(kernel, cycle, bands, panels, per_band),
            out_shape=jax.ShapeDtypeStruct((panels, bands, per_layer, tile, tile), jnp.bfloat16),
            in_specs=[hbm] * 4,
            out_specs=hbm,
            scratch_shapes=[
                pltpu.VMEM((cycle, message, tile), jnp.bfloat16),
                pltpu.VMEM((bands, message, tile), jnp.bfloat16),
                pltpu.VMEM((panels, band_blocks, tile, tile), jnp.float32),
                pltpu.VMEM((bands, panels, 8, tile), jnp.float32),
                pltpu.VMEM((bands, panels, per_layer, tile, tile), jnp.bfloat16),
                pltpu.SMEM((1, per_band, panels), jnp.int32),
                pltpu.SMEM(kept_rows.shape, jnp.int32),
                pltpu.VMEM(prune_mask.shape, jnp.int32),
                dma((5,)),
                dma((cycle // 2, panels)),
                dma((cycle // 2, panels)),
                dma((bands,)),
                dma((cycle, panels)),
                dma((bands,)),
                dma((bands,)),
                dma((bands,)),
                dma((bands, panels)),
                dma((bands, panels)),
                dma((panels,)),
            ],
            compiler_params=pltpu.CompilerParams(
                collective_id=0, has_side_effects=True, vmem_limit_bytes=63 * 1024 * 1024
            ),
        )(
            tile_values.reshape(panels * per_band * tile, tile),
            band_rows.transpose(1, 2, 0),
            kept_rows,
            prune_mask,
        )

    return jax.shard_map(
        per_device,
        mesh=mesh,
        in_specs=(
            P("blk", "layer", None, None, None),
            P("blk", "layer", None),
            P("blk", "layer", None),
            P("blk", None, None),
        ),
        out_specs=P("blk", None, "layer", None, None),
        check_vma=False,
    )
```
